256 devices in a mesh: pipe: 16 (over y_lo, x, core), expert: 16 (over y_hi, z).
Axes of the slice: x: 4, y: 4 (y_hi: 2, y_lo: 2; y = y_hi * 2 + y_lo), z: 8, core: 2. Of those that a mesh axis runs over, the one named last changes fastest.
Arguments:
- held_fwd: bfloat16 [16, 1024, 3584], P('pipe', 'expert'), may hold values from -6 to 6
- ids_fwd: int32 [16, 1024], P('pipe'), may hold values from 0 to 3, as said below
- probs_fwd: bfloat16 [16, 1024], P('pipe'), may hold values from 0.19921875 to 1
- saved_in: bfloat16 [16, 1024, 3584], P('pipe', 'expert'), may hold values from -6 to 6
- held_grad: bfloat16 [16, 1024, 3584], P('pipe', 'expert'), may hold values from -6 to 6
- ids_bwd: int32 [16, 1024], P('pipe'), may hold values from 0 to 3, as said below
- probs_bwd: bfloat16 [16, 1024], P('pipe'), may hold values from 0.19921875 to 1
- w_gate: bfloat16 [16, 3584, 6144], P('pipe', None, 'expert'), may hold values from -0.09375 to 0.09375
- w_up: bfloat16 [16, 3584, 6144], P('pipe', None, 'expert'), may hold values from -0.09375 to 0.09375
- w_down: bfloat16 [16, 6144, 3584], P('pipe', 'expert'), may hold values from -0.15625 to 0.15625
Outputs:
- fwd_out: bfloat16 [16, 1024, 3584], P('pipe', 'expert')
- grad_out: bfloat16 [16, 1024, 3584], P('pipe', 'expert')
The draws below stay inside these ranges and needn't reach their ends.
Inputs may be any that keep to these rules, and one draw needn't show every extreme that they name: `ids_fwd`: in every section one expert takes exactly 20 of the 64 rows of each device, 320 rows in all; no expert takes more than 20 of the rows of one device. `ids_bwd`: in every section one expert takes exactly 20 of the 64 rows of each device, 320 rows in all; no expert takes more than 20 of the rows of one device.
All inputs are finite; a program needn't handle non-finite values.
Results may differ from the reference program's by a relative error of at most 0.004.
Values may be sent and summed in bfloat16 or wider, within the bound.
A program may use at most 128 MiB of HBM per device.

```python
import jax
import jax.numpy as jnp
from jax import lax

D = 3584
FF = 1536
EXPERTS = 4
TOK_DEV = 64
SLOT = 20
TOKENS = 1024
CAP = 320
GROUP = 4
HID_DEV = 384
N_PIPE = 16
N_EXPERT = 16


def routing_table(key, stream):
    base_key = jax.random.fold_in(key, stream)
    key_busy, key_first, key_second, key_shuffle = jax.random.split(base_key, 4)
    busiest = jax.random.randint(key_busy, (N_PIPE, 1, 1), 0, EXPERTS)
    remain = TOK_DEV - SLOT
    count_shape = (N_PIPE, N_EXPERT, 1)
    first_low = max(0, remain - 2 * SLOT)
    first_high = min(SLOT, remain)
    first_count = jax.random.randint(key_first, count_shape, first_low, first_high + 1)
    second_low = jnp.maximum(0, remain - first_count - SLOT)
    second_high = jnp.minimum(SLOT, remain - first_count)
    second_count = jax.random.randint(key_second, count_shape, second_low, second_high + 1)
    position = jnp.arange(remain, dtype=jnp.int32)[None, None, :]
    others = (position >= first_count).astype(jnp.int32) + (position >= first_count + second_count).astype(jnp.int32)
    others = others + (others >= busiest).astype(jnp.int32)
    busy_rows = jnp.broadcast_to(busiest, (N_PIPE, N_EXPERT, SLOT))
    layout = jnp.concatenate([busy_rows, others], axis=2)
    key_list = jax.random.split(key_shuffle, N_PIPE * N_EXPERT)
    shuffle = jax.vmap(lambda single_key: jax.random.permutation(single_key, TOK_DEV))(key_list)
    shuffle = shuffle.reshape(N_PIPE, N_EXPERT, TOK_DEV)
    mixed = jnp.take_along_axis(layout, shuffle, axis=2)
    return mixed.reshape(N_PIPE, N_EXPERT * TOK_DEV).astype(jnp.int32)


def draw_ids_fwd(key, part):
    return routing_table(key, 11)


def draw_ids_bwd(key, part):
    return routing_table(key, 23)


def levels(own_key, extent, cuts, smallest, largest):
    level = 1.0
    for dim, blocks in cuts:
        heights = jax.random.uniform(jax.random.fold_in(jax.random.fold_in(own_key, 6), dim), (blocks,), jnp.float32, smallest / len(cuts), largest / len(cuts))
        level = level * jnp.repeat(jnp.exp(heights), extent[dim] // blocks).reshape((-1,) + (1,) * (len(extent) - 1 - dim))
    return level


def bell_draw(stream_key, dims, deviation, reach, cuts=(), held_as=jnp.bfloat16):
    values = jax.random.normal(stream_key, dims, jnp.float32) * deviation
    if len(cuts) > 0:
        values = levels(stream_key, dims, cuts, -0.22, 0.18) * values
    return jnp.clip(values, min=-reach, max=reach).astype(held_as)


def setup_inputs(seed: int = 0) -> dict:
    arg_keys = jax.random.split(jax.random.key(seed), 11)
    held_fwd = bell_draw(arg_keys[0], (N_PIPE, TOKENS, D), 1.0, 6.0, ((0, 16), (1, 16)))
    ids_fwd = draw_ids_fwd(jax.random.fold_in(arg_keys[10], 71), 0)
    probs_fwd = jnp.clip(0.19921875 + 0.80078125 * jax.random.uniform(arg_keys[2], (N_PIPE, TOKENS), jnp.float32) ** levels(arg_keys[2], (N_PIPE, TOKENS), ((0, 16),), -0.2, 0.2), 0.19921875, 1.0).astype(jnp.bfloat16)
    saved_in = bell_draw(arg_keys[3], (N_PIPE, TOKENS, D), 1.0, 6.0, ((0, 16), (1, 16)))
    held_grad = bell_draw(arg_keys[4], (N_PIPE, TOKENS, D), 1.0, 6.0, ((0, 16), (1, 16)))
    ids_bwd = draw_ids_bwd(jax.random.fold_in(arg_keys[10], 71), 0)
    probs_bwd = jnp.clip(0.19921875 + 0.80078125 * jax.random.uniform(arg_keys[6], (N_PIPE, TOKENS), jnp.float32) ** levels(arg_keys[6], (N_PIPE, TOKENS), ((0, 16),), -0.2, 0.2), 0.19921875, 1.0).astype(jnp.bfloat16)
    w_gate = bell_draw(arg_keys[7], (N_PIPE, D, EXPERTS * FF), D ** -0.5, 0.09375, ((0, 16), (2, 16)))
    w_up = bell_draw(arg_keys[8], (N_PIPE, D, EXPERTS * FF), D ** -0.5, 0.09375, ((0, 16), (2, 16)))
    w_down = bell_draw(arg_keys[9], (N_PIPE, EXPERTS * FF, D), FF ** -0.5, 0.15625, ((0, 16), (1, 16)))
    return dict(held_fwd=held_fwd, ids_fwd=ids_fwd, probs_fwd=probs_fwd, saved_in=saved_in, held_grad=held_grad, ids_bwd=ids_bwd, probs_bwd=probs_bwd, w_gate=w_gate, w_up=w_up, w_down=w_down)


def chosen_rows(routing, expert, capacity):
    matches = routing == expert
    places = jnp.nonzero(matches, size=capacity, fill_value=0)[0].astype(jnp.int32)
    filled = jnp.arange(capacity, dtype=jnp.int32) < jnp.sum(matches.astype(jnp.int32))
    return places, filled


def expert_forward(row_block, row_scale, gate_cols, up_cols, down_rows):
    gate_pre = jnp.dot(row_block, gate_cols, preferred_element_type=jnp.float32)
    upward = jnp.dot(row_block, up_cols, preferred_element_type=jnp.float32)
    hidden = (gate_pre * jax.nn.sigmoid(gate_pre) * upward).astype(jnp.bfloat16)
    return jnp.dot(hidden, down_rows, preferred_element_type=jnp.float32) * row_scale[:, None]


def expert_backward(row_block, grad_block, row_scale, gate_cols, up_cols, down_rows):
    gate_pre = jnp.dot(row_block, gate_cols, preferred_element_type=jnp.float32)
    upward = jnp.dot(row_block, up_cols, preferred_element_type=jnp.float32)
    d_hidden = jnp.dot(grad_block, down_rows.T, preferred_element_type=jnp.float32) * row_scale[:, None]
    sigmoid_gate = jax.nn.sigmoid(gate_pre)
    d_gate = (d_hidden * upward * sigmoid_gate * (1.0 + gate_pre * (1.0 - sigmoid_gate))).astype(jnp.bfloat16)
    d_up = (d_hidden * gate_pre * sigmoid_gate).astype(jnp.bfloat16)
    result = jnp.dot(d_gate, gate_cols.T, preferred_element_type=jnp.float32)
    return result + jnp.dot(d_up, up_cols.T, preferred_element_type=jnp.float32)


def rounded(number):
    return lax.optimization_barrier(number.astype(jnp.bfloat16)).astype(jnp.float32)


def one_section(inputs):
    x_rows, routing_f, weight_f, saved_rows, grad_rows, routing_b, weight_b, w_gate, w_up, w_down = inputs
    feature_width = x_rows.shape[1]
    fwd_total = jnp.zeros((TOKENS, feature_width), jnp.float32)
    bwd_total = jnp.zeros((TOKENS, feature_width), jnp.float32)
    for expert in range(EXPERTS):
        places, filled = chosen_rows(routing_f, expert, CAP)
        row_scale = jnp.where(filled, weight_f[places].astype(jnp.float32), 0.0)
        picked = x_rows[places]
        places_back, filled_back = chosen_rows(routing_b, expert, CAP)
        scale_back = jnp.where(filled_back, weight_b[places_back].astype(jnp.float32), 0.0)
        picked_back = saved_rows[places_back]
        grads_back = grad_rows[places_back]
        forward_sum = jnp.zeros((CAP, feature_width), jnp.float32)
        backward_sum = jnp.zeros((CAP, feature_width), jnp.float32)
        for tile_index in range(GROUP):
            first_unit = expert * FF + tile_index * HID_DEV
            gate_cols = w_gate[:, first_unit:first_unit + HID_DEV]
            up_cols = w_up[:, first_unit:first_unit + HID_DEV]
            down_rows = w_down[first_unit:first_unit + HID_DEV]
            forward_sum = forward_sum + rounded(expert_forward(picked, row_scale, gate_cols, up_cols, down_rows))
            backward_sum = backward_sum + rounded(expert_backward(picked_back, grads_back, scale_back, gate_cols, up_cols, down_rows))
        fwd_total = fwd_total.at[places].add(forward_sum)
        bwd_total = bwd_total.at[places_back].add(backward_sum)
    fwd_rows = (x_rows + fwd_total).astype(jnp.bfloat16)
    grad_out_rows = (grad_rows + bwd_total).astype(jnp.bfloat16)
    return fwd_rows, grad_out_rows


def reference(held_fwd, ids_fwd, probs_fwd, saved_in, held_grad, ids_bwd, probs_bwd, w_gate, w_up, w_down):
    incoming_rows = jnp.roll(held_fwd, 1, axis=0)
    incoming_grads = jnp.roll(held_grad, -1, axis=0)
    fwd_out, grad_out = lax.map(one_section, (incoming_rows, ids_fwd, probs_fwd, saved_in, incoming_grads, ids_bwd, probs_bwd, w_gate, w_up, w_down))
    return fwd_out, grad_out
```

```python
import functools

import jax
import jax.numpy as jnp
from jax import lax
from jax.experimental import pallas as pl
from jax.experimental.pallas import tpu as pltpu
from jax.sharding import PartitionSpec as P

EXPERTS = 4
SLOT = 20
MESH = pl.DeviceIdType.MESH
F32 = jnp.float32
BF16 = jnp.bfloat16

D = 3584
HID = 384
TOK = 64
PAIR = 2 * SLOT
HALF = D // 2
WIDE = 512
CHUNKS = [slice(c, c + WIDE) for c in range(0, D, WIDE)]
STEPS = 6

OTHER, PASS = 8, 9
RECV, HOME, TRANSIT = 8, 17, 18


def pick(q, values):
    result = jnp.int32(values[3])
    for i in (2, 1, 0):
        result = jnp.where(q == i, jnp.int32(values[i]), result)
    return result


def mirrored(index):
    return 7 - index if index < 8 else index


def out_plan(right, k):
    plan = []
    for q in range(4):
        place = q if right else 3 - q
        active, src, dst = False, 0, 0
        if place < 2 and k < place + 3:
            active, src = True, place - k + 2
            dst = src
        elif place == 2:
            active = True
            src, dst = (OTHER, PASS) if k == 0 else (5 - k, 5 - k)
        elif place == 3 and k < 2:
            active, src, dst = True, OTHER + k, 1 - k
        if not right:
            src, dst = mirrored(src), mirrored(dst)
        plan.append((active, src, dst))
    return plan


def back_plan(left, k):
    plan = []
    for q in range(4):
        place = q if left else 3 - q
        active, src, dst, added = False, 0, 0, -1
        if 3 - place <= k <= 4:
            index = k - 3 + place
            active = True
            src = index if left else 7 - index
            slot = RECV + index if left else 16 - index
            dst = slot if place > 0 else TRANSIT - index
            added = slot if place < 3 else -1
        elif place == 3 and k == 5:
            active, src, dst = True, TRANSIT, HOME
        plan.append((active, src, dst, added))
    return plan


def kernel(
    held_fwd,
    held_grad,
    saved,
    slot_f_row,
    slot_f_col,
    prob_f,
    slot_b_row,
    slot_b_col,
    prob_b,
    w_gate_hbm,
    w_up_hbm,
    w_down_hbm,
    out_f,
    out_b,
    w_gate,
    w_up,
    w_down,
    x_rows,
    g_rows,
    ysend,
    yrecv,
    blk,
    ret,
    ysend_back,
    yrecv_back,
    packed,
    packed_g,
    act_a,
    act_b,
    fin,
    w_sem,
    shift_send,
    shift_recv,
    y_send_sem,
    y_recv_sem,
    out_send_sem,
    out_recv_sem,
    back_send_sem,
    back_recv_sem,
):
    pipe = lax.axis_index("pipe")
    position = lax.axis_index("expert")
    plane = position // 8
    z = position % 8
    half = z // 4
    q = z % 4
    right = (pipe, plane * 8 + (z + 1) % 8)
    left = (pipe, plane * 8 + (z + 7) % 8)
    across = (pipe, (1 - plane) * 8 + z)
    after = ((pipe + 1) % 16, position)
    before = ((pipe + 15) % 16, position)

    weight_copies = [
        pltpu.make_async_copy(w_gate_hbm, w_gate, w_sem.at[0]),
        pltpu.make_async_copy(w_up_hbm, w_up, w_sem.at[1]),
        pltpu.make_async_copy(w_down_hbm, w_down, w_sem.at[2]),
    ]
    for copy in weight_copies:
        copy.start()

    barrier = pltpu.get_barrier_semaphore()
    for device in (right, left, across, after, before):
        pl.semaphore_signal(barrier, inc=1, device_id=device, device_id_type=MESH)
    pl.semaphore_wait(barrier, 5)

    def remote(src, dst, send_sem, recv_sem, device):
        return pltpu.make_async_remote_copy(
            src_ref=src,
            dst_ref=dst,
            send_sem=send_sem,
            recv_sem=recv_sem,
            device_id=device,
            device_id_type=MESH,
        )

    shift_g = remote(held_grad, g_rows, shift_send.at[0], shift_recv.at[0], before)
    shift_x = remote(held_fwd, x_rows, shift_send.at[1], shift_recv.at[1], after)
    shift_g.start()
    shift_x.start()

    def grid(rows, cols):
        return (
            lax.broadcasted_iota(jnp.int32, (rows, cols), 0),
            lax.broadcasted_iota(jnp.int32, (rows, cols), 1),
        )

    def hot(mask):
        return jnp.where(mask, jnp.float32(1), jnp.float32(0)).astype(BF16)

    def dot(a, b):
        return jnp.dot(a, b, preferred_element_type=F32)

    def dot_t(a, b):
        return lax.dot_general(a, b, (((1,), (1,)), ((), ())), preferred_element_type=F32)

    sources = (saved, g_rows, x_rows)
    slot_rows = (slot_b_row, slot_b_row, slot_f_row)

    def y_copy(t):
        return remote(ysend.at[t], yrecv.at[t], y_send_sem.at[t], y_recv_sem.at[t], across)

    def send_across(t):
        row, _ = grid(PAIR, TOK)
        chosen = hot(row + (1 - plane) * PAIR == slot_rows[t][...])
        for c in CHUNKS:
            ysend[t, :, c] = dot(chosen, sources[t][:, c]).astype(BF16)
        y_copy(t).start()

    def build(t):
        y_copy(t).wait_recv()
        row, _ = grid(PAIR, TOK)
        to, frm = grid(PAIR, PAIR)
        for line, place in ((half, q + 2), (1 - half, OTHER)):
            own = hot((row < SLOT) & (row + (2 * plane + line) * SLOT == slot_rows[t][...]))
            theirs = hot((to >= SLOT) & (frm == to - SLOT + SLOT * line))
            for c in CHUNKS:
                value = dot(own, sources[t][:, c]) + dot(theirs, yrecv[t, :, c])
                blk[t, place, :, c] = value.astype(BF16)

    def out_copy(t, going_right, k, src, dst):
        way = 0 if going_right else 1
        return remote(
            blk.at[t, src],
            blk.at[t, dst],
            out_send_sem.at[t, way, k],
            out_recv_sem.at[t, dst],
            right if going_right else left,
        )

    def out_send(t, k, finish=False):
        for going_right in (True, False):
            plan = out_plan(going_right, k)
            if not any(p[0] for p in plan):
                continue
            active, src, dst = (pick(q, [int(p[i]) for p in plan]) for i in range(3))

            @pl.when(active == 1)
            def _():
                copy = out_copy(t, going_right, k, src, dst)
                if finish:
                    copy.wait_send()
                else:
                    copy.start()

    def out_arrive(t, k):
        for going_right in (True, False):
            plan = out_plan(going_right, k)
            plan = [plan[(i - 1) % 4] if going_right else plan[(i + 1) % 4] for i in range(4)]
            active, _, dst = (pick(q, [int(p[i]) for p in plan]) for i in range(3))

            @pl.when(active == 1)
            def _():
                out_copy(t, going_right, k, dst, dst).wait_recv()

    def cols(part):
        return pl.ds(part * HALF, HALF)

    def back_copy(t, part, going_left, k, src, dst):
        way = 0 if going_left else 1
        return remote(
            ret.at[t, src, :, cols(part)],
            ret.at[t, dst, :, cols(part)],
            back_send_sem.at[t, part, way, k],
            back_recv_sem.at[t, part, dst],
            left if going_left else right,
        )

    def back_send(t, part, k, finish=False):
        for going_left in (True, False):
            plan = back_plan(going_left, k)
            active, src, dst, added = (pick(q, [int(p[i]) for p in plan]) for i in range(4))
            if not finish and any(p[3] >= 0 for p in plan):

                @pl.when((active == 1) & (added >= 0))
                def _():
                    total = ret[t, src, :, cols(part)].astype(F32)
                    total = total + ret[t, added, :, cols(part)].astype(F32)
                    ret[t, src, :, cols(part)] = total.astype(BF16)

            @pl.when(active == 1)
            def _():
                copy = back_copy(t, part, going_left, k, src, dst)
                if finish:
                    copy.wait_send()
                else:
                    copy.start()

    def back_arrive(t, part, k):
        for going_left in (True, False):
            plan = back_plan(going_left, k)
            plan = [plan[(i + 1) % 4] if going_left else plan[(i - 1) % 4] for i in range(4)]
            active, _, dst, _ = (pick(q, [int(p[i]) for p in plan]) for i in range(4))

            @pl.when(active == 1)
            def _():
                back_copy(t, part, going_left, k, dst, dst).wait_recv()

    def pack(t, to):
        for c in CHUNKS:
            rows = [blk[t, i, :, c].astype(F32) for i in range(8)]
            to[:, c] = jnp.concatenate(rows, axis=0).astype(BF16)

    def spread(t, c, value):
        for i in range(8):
            ret[t, i, :, c] = value[i * PAIR : (i + 1) * PAIR].astype(BF16)

    def hidden_bwd():
        pack(0, packed)
        pack(1, packed_g)
        gate = dot(packed[...], w_gate[...])
        up = dot(packed[...], w_up[...])
        dh = dot_t(packed_g[...], w_down[...])
        s = jax.nn.sigmoid(gate)
        act_a[...] = (dh * up * s * (1.0 + gate * (1.0 - s))).astype(BF16)
        act_b[...] = (dh * gate * s).astype(BF16)

    def rows_bwd(chunks):
        for c in chunks:
            spread(0, c, dot_t(act_a[...], w_gate[c, :]) + dot_t(act_b[...], w_up[c, :]))

    def hidden_fwd():
        pack(2, packed)
        gate = dot(packed[...], w_gate[...])
        up = dot(packed[...], w_up[...])
        act_a[...] = (gate * jax.nn.sigmoid(gate) * up).astype(BF16)

    def rows_fwd(chunks):
        for c in chunks:
            spread(1, c, dot(act_a[...], w_down[:, c]))

    def y_back_copy(t):
        return remote(
            ysend_back.at[t], yrecv_back.at[t], y_send_sem.at[3 + t], y_recv_sem.at[3 + t], across
        )

    def finish_home(t):
        for c in CHUNKS:
            fin[t, 0, :, c] = ret[t, q + 2, :, c].astype(F32)
            fin[t, 1, :, c] = ret[t, HOME, :, c].astype(F32)

        @pl.when(q < 3)
        def _():
            for c in CHUNKS:
                fin[t, 0, :, c] += ret[t, RECV + q + 2, :, c].astype(F32)

        @pl.when(q > 0)
        def _():
            for c in CHUNKS:
                fin[t, 0, :, c] += ret[t, RECV + q + 3, :, c].astype(F32)

        to, frm = grid(PAIR, PAIR)
        main = hot((frm >= SLOT) & (to == frm - SLOT + SLOT * half))
        other = hot((frm >= SLOT) & (to == frm - SLOT + SLOT * (1 - half)))
        for c in CHUNKS:
            value = dot(main, fin[t, 0, :, c].astype(BF16))
            value = value + dot(other, fin[t, 1, :, c].astype(BF16))
            ysend_back[t, :, c] = value.astype(BF16)
        y_back_copy(t).start()

    def combine(t, base, slot_col, prob, out):
        y_back_copy(t).wait_recv()
        _, col = grid(TOK, PAIR)
        slots = slot_col[...]
        main = hot((col < SLOT) & (slots == (2 * plane + half) * SLOT + col))
        other = hot((col < SLOT) & (slots == (2 * plane + 1 - half) * SLOT + col))
        theirs = hot(slots == (1 - plane) * PAIR + col)
        scale = prob[...]
        for c in CHUNKS:
            value = dot(main, fin[t, 0, :, c].astype(BF16))
            value = value + dot(other, fin[t, 1, :, c].astype(BF16))
            value = value + dot(theirs, yrecv_back[t, :, c])
            out[:, c] = (base[:, c].astype(F32) + scale * value).astype(BF16)

    send_across(0)
    shift_g.wait_recv()
    send_across(1)
    build(0)
    out_send(0, 0)
    build(1)
    out_send(1, 0)
    shift_x.wait_recv()
    send_across(2)
    for k in range(1, STEPS):
        out_arrive(0, k - 1)
        out_send(0, k)
        out_arrive(1, k - 1)
        out_send(1, k)
    out_arrive(0, STEPS - 1)
    build(2)
    out_send(2, 0)
    for copy in weight_copies:
        copy.wait()
    out_arrive(1, STEPS - 1)

    hidden_bwd()
    out_arrive(2, 0)
    out_send(2, 1)
    rows_bwd(CHUNKS)
    back_send(0, 0, 0)
    back_send(0, 1, 0)
    for k in range(1, STEPS):
        out_arrive(2, k)
        if k + 1 < STEPS:
            out_send(2, k + 1)
        for part in (0, 1):
            back_arrive(0, part, k - 1)
            back_send(0, part, k)
    hidden_fwd()
    rows_fwd(CHUNKS)
    back_send(1, 0, 0)
    back_send(1, 1, 0)
    for part in (0, 1):
        back_arrive(0, part, STEPS - 1)
    finish_home(0)
    for k in range(1, STEPS):
        for part in (0, 1):
            back_arrive(1, part, k - 1)
            back_send(1, part, k)
        if k == 2:
            combine(0, g_rows, slot_b_col, prob_b, out_b)
    for part in (0, 1):
        back_arrive(1, part, STEPS - 1)
    finish_home(1)
    combine(1, x_rows, slot_f_col, prob_f, out_f)

    shift_g.wait_send()
    shift_x.wait_send()
    for t in range(3):
        y_copy(t).wait_send()
        for k in range(STEPS):
            out_send(t, k, finish=True)
    for t in range(2):
        y_back_copy(t).wait_send()
        for part in (0, 1):
            for k in range(STEPS):
                back_send(t, part, k, finish=True)


def slots_of(ids, probs, position):
    own = lax.dynamic_slice_in_dim(ids.reshape(-1, TOK), position, 1)[0]
    prob = lax.dynamic_slice_in_dim(probs.reshape(-1, TOK), position, 1)[0]
    place = jnp.arange(TOK)
    earlier = (own[None, :] == own[:, None]) & (place[None, :] < place[:, None])
    slot = own * SLOT + jnp.sum(earlier.astype(jnp.int32), axis=1)
    return slot[None, :], slot[:, None], prob.astype(F32)[:, None]


def on_device(
    held_fwd, ids_fwd, probs_fwd, saved_in, held_grad, ids_bwd, probs_bwd, w_gate, w_up, w_down
):
    position = lax.axis_index("expert")
    forward = slots_of(ids_fwd[0], probs_fwd[0], position)
    backward = slots_of(ids_bwd[0], probs_bwd[0], position)
    vmem = pl.BlockSpec(memory_space=pltpu.VMEM)
    hbm = pl.BlockSpec(memory_space=pl.ANY)
    rows = jax.ShapeDtypeStruct((TOK, D), BF16)
    fwd, grad = pl.pallas_call(
        kernel,
        out_shape=(rows, rows),
        in_specs=[vmem] * 9 + [hbm] * 3,
        out_specs=(vmem, vmem),
        scratch_shapes=[
            pltpu.VMEM((D, HID), BF16),
            pltpu.VMEM((D, HID), BF16),
            pltpu.VMEM((HID, D), BF16),
            pltpu.VMEM((TOK, D), BF16),
            pltpu.VMEM((TOK, D), BF16),
            pltpu.VMEM((3, PAIR, D), BF16),
            pltpu.VMEM((3, PAIR, D), BF16),
            pltpu.VMEM((3, 10, PAIR, D), BF16),
            pltpu.VMEM((2, 19, PAIR, D), BF16),
            pltpu.VMEM((2, PAIR, D), BF16),
            pltpu.VMEM((2, PAIR, D), BF16),
            pltpu.VMEM((8 * PAIR, D), BF16),
            pltpu.VMEM((8 * PAIR, D), BF16),
            pltpu.VMEM((8 * PAIR, HID), BF16),
            pltpu.VMEM((8 * PAIR, HID), BF16),
            pltpu.VMEM((2, 2, PAIR, D), F32),
            pltpu.SemaphoreType.DMA((3,)),
            pltpu.SemaphoreType.DMA((2,)),
            pltpu.SemaphoreType.DMA((2,)),
            pltpu.SemaphoreType.DMA((5,)),
            pltpu.SemaphoreType.DMA((5,)),
            pltpu.SemaphoreType.DMA((3, 2, STEPS)),
            pltpu.SemaphoreType.DMA((3, 10)),
            pltpu.SemaphoreType.DMA((2, 2, 2, STEPS)),
            pltpu.SemaphoreType.DMA((2, 2, 19)),
        ],
        compiler_params=pltpu.CompilerParams(
            collective_id=0, has_side_effects=True, vmem_limit_bytes=60 * 2**20
        ),
        cost_estimate=pl.CostEstimate(
            flops=7_050_000_000, bytes_accessed=12_000_000, transcendentals=300_000
        ),
        name="relay_experts",
    )(held_fwd[0], held_grad[0], saved_in[0], *forward, *backward, w_gate[0], w_up[0], w_down[0])
    return (fwd[None], grad[None])


def solution(mesh):
    return jax.shard_map(
        on_device,
        mesh=mesh,
        in_specs=(
            P("pipe", "expert", None),
            P("pipe", None),
            P("pipe", None),
            P("pipe", "expert", None),
            P("pipe", "expert", None),
            P("pipe", None),
            P("pipe", None),
            P("pipe", None, "expert"),
            P("pipe", None, "expert"),
            P("pipe", "expert", None),
        ),
        out_specs=(P("pipe", "expert", None), P("pipe", "expert", None)),
        check_vma=False,
    )
```

```python
import jax
import jax.numpy as jnp
from jax import lax
from jax.experimental import pallas as pl
from jax.experimental.pallas import tpu as pltpu
from jax.sharding import PartitionSpec as P

SLOT = 20
MESH = pl.DeviceIdType.MESH
F32 = jnp.float32
BF16 = jnp.bfloat16

D = 3584
HID = 384
TOK = 64
ROWS = 2 * SLOT
HALF = D // 2
WIDE = 256
STARTS = tuple(range(0, HALF, WIDE))
ALL = 8 * SLOT
STEPS = 6

OTHER, PASS = 8, 9
RECV, HOME, TRANSIT = 8, 17, 18
S_A, G_A, S_B, G_B, X_B, X_A = range(6)
R_A, R_B, F_B, F_A = range(4)
PARTS = (1, 1, 1, 2)
DEPTH = 3

ORDER = (
    (
        (),
        (),
        ((0, 0, 0), (0, 1, 0)),
        ((0, 0, 1), (0, 1, 1), (2, 0, 0), (2, 1, 0), (0, 0, 2)),
        ((1, 0, 0), (1, 1, 0), (2, 0, 1), (1, 0, 1), (3, 1, 0), (2, 1, 1)),
        ((3, 0, 0), (5, 1, 0), (3, 0, 1), (2, 0, 2), (1, 1, 1), (4, 0, 0), (4, 1, 0)),
        ((5, 0, 0), (1, 0, 2), (4, 0, 1), (5, 0, 1), (3, 1, 1)),
        (),
        ((3, 0, 2),),
        (),
        (),
        (),
        (),
        (),
        (),
        (),
        (),
        ((6, 1, 0), (6, 1, 1)),
        ((6, 1, 2), (6, 1, 3), (4, 1, 1), (6, 1, 4)),
        (),
        ((4, 0, 2),),
        (),
        (),
        (),
        (),
        (),
        (),
        (),
        (),
        ((8, 1, 0), (8, 1, 1), (8, 1, 2), (8, 1, 3), (5, 1, 1), (8, 1, 4), (5, 0, 2)),
        (),
        (),
        (),
        (),
        (),
        ((8, 0, 3),),
        (),
        (),
        (),
        ((10, 1, 0), (10, 1, 1), (8, 0, 4), (10, 1, 2)),
        ((8, 1, 5), (10, 1, 3), (10, 1, 4)),
        (),
        (),
        (),
        (),
        (),
        ((10, 0, 3),),
        ((12, 1, 0), (12, 1, 1)),
        (),
        (),
        ((10, 0, 4), (13, 1, 0), (13, 1, 1), (10, 1, 5), (12, 1, 2)),
        (),
        ((6, 0, 3), (13, 1, 2), (6, 0, 4), (12, 1, 3), (13, 1, 3), (6, 1, 5), (12, 1, 4), (12, 0, 3)),
        ((13, 0, 3), (12, 0, 4), (13, 1, 4)),
        ((13, 0, 4), (12, 1, 5), (13, 1, 5)),
        (),
    ),
    (
        (),
        (),
        ((0, 0, 0), (0, 1, 0), (0, 1, 1)),
        ((0, 0, 1), (0, 1, 2), (2, 0, 0), (2, 1, 1), (0, 0, 2)),
        ((0, 1, 3), (1, 0, 0), (2, 1, 0), (2, 0, 1), (0, 1, 4), (0, 0, 3), (2, 1, 2)),
        ((2, 0, 2), (1, 1, 0), (1, 0, 1)),
        ((0, 1, 5), (1, 0, 2), (2, 1, 3), (3, 0, 0), (1, 1, 1), (3, 0, 1), (2, 1, 4), (2, 0, 3), (1, 1, 2), (3, 0, 2), (1, 1, 3), (4, 0, 0), (2, 1, 5), (1, 0, 3), (1, 1, 4), (4, 0, 1), (3, 1, 0), (4, 0, 2)),
        ((1, 1, 5),),
        (),
        ((5, 0, 0),),
        (),
        ((3, 1, 1),),
        (),
        (),
        ((5, 0, 1),),
        (),
        (),
        ((3, 1, 2),),
        ((5, 0, 2), (3, 1, 3), (3, 1, 4), (3, 0, 3), (4, 1, 0)),
        ((3, 1, 5), (6, 1, 1)),
        (),
        (),
        ((4, 1, 1), (6, 1, 2)),
        (),
        (),
        (),
        (),
        ((6, 1, 3), (4, 1, 2)),
        (),
        ((6, 1, 4), (4, 1, 3), (4, 1, 4), (4, 0, 3), (5, 1, 0), (8, 1, 1), (5, 1, 1)),
        (),
        (),
        ((8, 1, 2), (4, 1, 5)),
        (),
        (),
        (),
        (),
        (),
        ((8, 1, 3), (8, 0, 2)),
        ((8, 1, 4), (8, 0, 3), (8, 0, 4), (5, 0, 3), (5, 1, 2), (5, 1, 3), (10, 1, 1), (5, 1, 4), (10, 1, 2), (5, 1, 5), (10, 1, 3), (10, 0, 2)),
        (),
        (),
        ((10, 0, 3),),
        ((10, 1, 4),),
        (),
        (),
        (),
        ((10, 0, 4),),
        (),
        (),
        ((6, 0, 2), (12, 1, 1), (6, 0, 3), (12, 1, 2), (13, 1, 1), (6, 0, 4), (13, 1, 2), (12, 0, 2)),
        (),
        ((12, 1, 3), (13, 0, 2), (13, 1, 3), (12, 0, 3), (12, 1, 4), (13, 0, 3), (13, 1, 4), (12, 0, 4), (13, 0, 4)),
        (),
        (),
        (),
    ),
    (
        (),
        (),
        ((0, 0, 0), (0, 1, 0), (0, 0, 1)),
        ((0, 0, 2), (0, 1, 1), (2, 1, 0), (2, 0, 1), (0, 1, 2)),
        ((0, 0, 3), (1, 1, 0), (2, 0, 0), (2, 1, 1), (0, 0, 4), (0, 1, 3), (2, 0, 2)),
        ((2, 1, 2), (1, 0, 0), (1, 1, 1)),
        ((0, 0, 5), (1, 1, 2), (2, 0, 3), (3, 1, 0), (1, 0, 1), (3, 1, 1), (2, 0, 4), (2, 1, 3), (1, 0, 2), (3, 1, 2), (1, 0, 3), (4, 1, 0), (2, 0, 5), (1, 1, 3), (1, 0, 4), (4, 1, 1), (3, 0, 0), (4, 1, 2)),
        ((1, 0, 5),),
        (),
        ((5, 1, 0),),
        (),
        ((3, 0, 1),),
        (),
        (),
        ((5, 1, 1),),
        (),
        (),
        ((3, 0, 2),),
        ((5, 1, 2), (3, 0, 3), (3, 0, 4), (3, 1, 3), (4, 0, 0)),
        ((3, 0, 5), (6, 0, 1)),
        (),
        (),
        ((4, 0, 1), (6, 0, 2)),
        (),
        (),
        (),
        (),
        ((6, 0, 3), (4, 0, 2)),
        (),
        ((6, 0, 4), (4, 0, 3), (4, 0, 4), (4, 1, 3), (5, 0, 0), (8, 0, 1), (5, 0, 1)),
        (),
        ((8, 0, 2), (4, 0, 5)),
        (),
        (),
        (),
        (),
        (),
        (),
        ((8, 1, 2), (8, 0, 3)),
        ((8, 0, 4), (8, 1, 3), (8, 1, 4), (5, 1, 3), (5, 0, 2), (5, 0, 3), (10, 0, 1), (5, 0, 4), (10, 0, 2), (5, 0, 5), (10, 0, 3), (10, 1, 2)),
        (),
        (),
        ((10, 1, 3),),
        ((10, 0, 4),),
        (),
        (),
        (),
        ((10, 1, 4),),
        (),
        (),
        ((6, 1, 2), (12, 0, 1), (6, 1, 3), (12, 0, 2), (13, 0, 1), (6, 1, 4), (13, 0, 2), (12, 1, 2)),
        (),
        ((12, 0, 3), (13, 1, 2), (13, 0, 3), (12, 1, 3), (12, 0, 4), (13, 1, 3), (13, 0, 4), (12, 1, 4), (13, 1, 4)),
        (),
        (),
        (),
    ),
    (
        (),
        (),
        ((0, 0, 0), (0, 1, 0)),
        ((0, 0, 1), (0, 1, 1), (2, 1, 0), (2, 0, 0), (0, 1, 2)),
        ((1, 0, 0), (1, 1, 0), (2, 1, 1), (1, 1, 1), (3, 0, 0), (2, 0, 1)),
        ((3, 1, 0), (5, 0, 0), (3, 1, 1), (2, 1, 2), (1, 0, 1), (4, 1, 0), (4, 0, 0)),
        ((5, 1, 0), (1, 1, 2), (4, 1, 1), (5, 1, 1), (3, 0, 1)),
        (),
        ((3, 1, 2),),
        (),
        (),
        (),
        (),
        (),
        (),
        (),
        (),
        ((6, 0, 0), (6, 0, 1)),
        ((6, 0, 2), (6, 0, 3), (4, 0, 1), (6, 0, 4)),
        (),
        ((4, 1, 2),),
        (),
        (),
        (),
        (),
        (),
        (),
        (),
        (),
        ((8, 0, 0), (8, 0, 1), (8, 0, 2), (8, 0, 3), (5, 0, 1), (8, 0, 4), (5, 1, 2)),
        (),
        (),
        (),
        (),
        (),
        ((8, 1, 3),),
        (),
        (),
        (),
        ((10, 0, 0), (10, 0, 1), (8, 1, 4), (10, 0, 2)),
        ((8, 0, 5), (10, 0, 3), (10, 0, 4)),
        (),
        (),
        (),
        (),
        (),
        ((10, 1, 3),),
        ((12, 0, 0), (12, 0, 1)),
        (),
        (),
        ((10, 1, 4), (13, 0, 0), (13, 0, 1), (10, 0, 5), (12, 0, 2)),
        (),
        ((6, 1, 3), (13, 0, 2), (6, 1, 4), (12, 0, 3), (13, 0, 3), (6, 0, 5), (12, 0, 4), (12, 1, 3)),
        ((13, 1, 3), (12, 1, 4), (13, 0, 4)),
        ((13, 1, 4), (12, 0, 5), (13, 0, 5)),
        (),
    ),
)


def mirrored(index):
    return 7 - index if index < 8 else index


def out_plan(right, k):
    plan = []
    for q in range(4):
        place = q if right else 3 - q
        active, src, dst = False, 0, 0
        if place < 2 and k < place + 3:
            active, src = True, place - k + 2
            dst = src
        elif place == 2:
            active = True
            src, dst = (OTHER, PASS) if k == 0 else (5 - k, 5 - k)
        elif place == 3 and k < 2:
            active, src, dst = True, OTHER + k, 1 - k
        if not right:
            src, dst = mirrored(src), mirrored(dst)
        plan.append((active, src, dst))
    return plan


def back_plan(left, k):
    plan = []
    for q in range(4):
        place = q if left else 3 - q
        active, src, dst, added = False, 0, 0, -1
        if 3 - place <= k <= 4:
            index = k - 3 + place
            active = True
            src = index if left else 7 - index
            slot = RECV + index if left else 16 - index
            dst = slot if place > 0 else TRANSIT - index
            added = slot if place < 3 else -1
        elif place == 3 and k == 5:
            active, src, dst = True, TRANSIT, HOME
        plan.append((active, src, dst, added))
    return plan


def kernel(
    held_fwd,
    held_grad,
    saved,
    ids_f,
    probs_f,
    ids_b,
    probs_b,
    w_gate_hbm,
    w_up_hbm,
    w_down_hbm,
    out_f,
    out_b,
    w_gate,
    w_up,
    w_down,
    x_rows,
    g_rows,
    y_out,
    y_back,
    blk,
    ret,
    lhs,
    act,
    pre,
    total,
    gathering,
    scattering,
    w_sem,
    shift_send,
    shift_recv,
    y_send_sem,
    y_recv_sem,
    out_send_sem,
    out_recv_sem,
    back_send_sem,
    back_recv_sem,
):
    pipe = lax.axis_index("pipe")
    position = lax.axis_index("expert")
    plane = position // 8
    z = position % 8
    half = z // 4
    q = z % 4
    right = (pipe, plane * 8 + (z + 1) % 8)
    left = (pipe, plane * 8 + (z + 7) % 8)
    across = (pipe, (1 - plane) * 8 + z)
    after = ((pipe + 1) % 16, position)
    before = ((pipe + 15) % 16, position)

    barrier = pltpu.get_barrier_semaphore()
    for device in (right, left, across, after, before):
        pl.semaphore_signal(barrier, inc=1, device_id=device, device_id_type=MESH)

    weight_copies = [
        pltpu.make_async_copy(w_gate_hbm, w_gate, w_sem.at[0]),
        pltpu.make_async_copy(w_up_hbm, w_up, w_sem.at[1]),
        pltpu.make_async_copy(w_down_hbm, w_down, w_sem.at[2]),
    ]
    for copy in weight_copies:
        copy.start()

    def remote(src, dst, send_sem, recv_sem, device):
        return pltpu.make_async_remote_copy(
            src_ref=src,
            dst_ref=dst,
            send_sem=send_sem,
            recv_sem=recv_sem,
            device_id=device,
            device_id_type=MESH,
        )

    def grid(rows, cols):
        return (
            lax.broadcasted_iota(jnp.int32, (rows, cols), 0),
            lax.broadcasted_iota(jnp.int32, (rows, cols), 1),
        )

    def hot(mask):
        return jnp.where(mask, jnp.float32(1), jnp.float32(0)).astype(BF16)

    def dot(a, b):
        return jnp.dot(a, b, preferred_element_type=F32)

    def dot_t(a, b):
        return lax.dot_general(a, b, (((1,), (1,)), ((), ())), preferred_element_type=F32)

    def own_part(ref):
        base = pl.multiple_of((position // 2) * 128, 128)
        both = ref[:, pl.ds(base, 128)].astype(F32)
        return jnp.where(position % 2 == 0, both[:, :TOK], both[:, TOK:])

    def upright(row):
        i, j = grid(TOK, TOK)
        return jnp.sum(jnp.where(i == j, row, jnp.float32(0)), axis=1, keepdims=True)

    def routing(ids_ref, probs_ref):
        row = own_part(ids_ref)
        col = upright(row)
        i, j = grid(TOK, TOK)
        one, none = jnp.float32(1), jnp.float32(0)
        rank_row = jnp.sum(jnp.where((row == col) & (i < j), one, none), axis=0, keepdims=True)
        rank_col = jnp.sum(jnp.where((row == col) & (j < i), one, none), axis=1, keepdims=True)
        return row * SLOT + rank_row, col * SLOT + rank_col, upright(own_part(probs_ref))

    sources = (saved, g_rows, x_rows)

    def choose(t, slot_row):
        side = (S_A, G_A, X_A)[t]
        targets = (
            (2 * plane + half, blk.at[side, q + 2]),
            (2 * plane + 1 - half, blk.at[side, OTHER]),
            (2 * (1 - plane) + half, y_out.at[t, 0]),
            (2 * (1 - plane) + 1 - half, y_out.at[t, 1]),
        )
        i, j = grid(ROWS, 2 * TOK)
        slots = jnp.concatenate([slot_row, slot_row], axis=1)
        slots = jnp.where((i < SLOT) == (j < TOK), slots, jnp.float32(-1))
        offset = jnp.where(i < SLOT, i, i - SLOT)
        maps = [
            jnp.where((offset + expert * SLOT).astype(F32) == slots, jnp.float32(1), jnp.float32(0))
            for expert, _ in targets
        ]
        maps = jnp.concatenate(maps, axis=0).astype(BF16)
        for c in STARTS:
            upper = sources[t][:, c : c + WIDE]
            lower = sources[t][:, HALF + c : HALF + c + WIDE]
            value = dot(maps, jnp.concatenate([upper, lower], axis=0))
            for n in range(4):
                targets[n][1][:, c : c + WIDE] = value[n * ROWS : (n + 1) * ROWS].astype(BF16)

    def y_copy(t, n):
        side = (S_B, G_B, X_B)[t]
        place = q + 2 if n == 0 else OTHER
        return remote(
            y_out.at[t, n], blk.at[side, place], y_send_sem.at[t, n], y_recv_sem.at[t, n], across
        )

    def columns(t, p):
        if PARTS[t] == 1:
            return pl.ds(0, HALF)
        return pl.ds(0, 4 * WIDE) if p == 0 else pl.ds(4 * WIDE, 3 * WIDE)

    def out_copy(t, way, k, src, dst):
        return remote(
            blk.at[t, src],
            blk.at[t, dst],
            out_send_sem.at[t, way, k],
            out_recv_sem.at[t, dst],
            right if way == 0 else left,
        )

    def back_copy(t, p, way, k, src, dst):
        return remote(
            ret.at[t, src, :, columns(t, p)],
            ret.at[t, dst, :, columns(t, p)],
            back_send_sem.at[t, p, way, k],
            back_recv_sem.at[t, p, dst],
            left if way == 0 else right,
        )

    arrived = [set() for _ in range(4)]
    started = [([], []) for _ in range(4)]

    def need(place, key):
        if key in arrived[place]:
            return
        arrived[place].add(key)
        if key[0] == "out":
            out_copy(key[1], 0, 0, key[2], key[2]).wait_recv()
        elif key[0] == "back":
            back_copy(key[1], key[2], 0, 0, key[3], key[3]).wait_recv()
        elif key[1] in (S_B, G_B, X_B):
            y_copy((S_B, G_B, X_B).index(key[1]), key[2]).wait_recv()

    def described(place, op):
        stream, way, k = op
        if stream < 6:
            _, src, dst = out_plan(way == 0, k)[place]
            return out_copy(stream, way, k, src, dst)
        t, p = (stream - 6) // 2, (stream - 6) % 2
        _, src, dst, _ = back_plan(way == 0, k)[place]
        return back_copy(t, p, way, k, src, dst)

    def start(place, op):
        stream, way, k = op
        if stream < 6:
            _, src, _ = out_plan(way == 0, k)[place]
            if src == place + 2:
                need(place, ("own", stream, 0))
            elif src == OTHER:
                need(place, ("own", stream, 1))
            else:
                need(place, ("out", stream, src))
        else:
            t, p = (stream - 6) // 2, (stream - 6) % 2
            _, src, _, added = back_plan(way == 0, k)[place]
            if src == TRANSIT:
                need(place, ("back", t, p, TRANSIT))
            if added >= 0:
                need(place, ("back", t, p, added))
                cols = columns(t, p)
                joined = ret[t, src, :, cols].astype(F32) + ret[t, added, :, cols].astype(F32)
                ret[t, src, :, cols] = joined.astype(BF16)
        link = started[place][(way == 0) == (stream < 6)]
        if len(link) >= DEPTH:
            described(place, link[-DEPTH]).wait_send()
        link.append(op)
        described(place, op).start()

    def all_of(*sides):
        def keys(place):
            found = []
            for side in sides:
                found.append(("own", side, 0))
                found += [("out", side, i) for i in range(8) if i != place + 2]
            return found

        return keys

    def home_of(t, parts):
        def keys(place):
            found = []
            for p in parts:
                found.append(("back", t, p, HOME))
                if place < 3:
                    found.append(("back", t, p, RECV + place + 2))
                if place > 0:
                    found.append(("back", t, p, RECV + place + 3))
            return found

        return keys

    def nothing(place):
        return []

    count = [0]

    def piece(keys=nothing):
        number = count[0]
        count[0] += 1
        for place in range(4):
            ops = ORDER[place][number]
            if ops or any(key not in arrived[place] for key in keys(place)):

                @pl.when(q == place)
                def _():
                    for op in ops:
                        start(place, op)
                    for key in keys(place):
                        need(place, key)

    def gather(t, to):
        for c in STARTS:
            rows = [blk[t, i, :, c : c + WIDE].astype(F32) for i in range(8)]
            value = dot(gathering[...], jnp.concatenate(rows, axis=0).astype(BF16)).astype(BF16)
            lhs[to, :, c : c + WIDE] = value[:ALL]
            lhs[to, :, HALF + c : HALF + c + WIDE] = value[ALL:]

    def scatter(t, c, upper, lower):
        both = jnp.concatenate([upper, lower], axis=0).astype(BF16)
        value = dot(scattering[...], both)
        for i in range(8):
            ret[t, i, :, c : c + WIDE] = value[i * ROWS : (i + 1) * ROWS].astype(BF16)

    def hidden_bwd():
        pre[0] = dot(lhs[0], w_gate[...])
        piece()
        pre[1] = dot(lhs[0], w_up[...])
        piece()
        dh = dot_t(lhs[1], w_down[...])
        gate, up = pre[0], pre[1]
        s = jax.nn.sigmoid(gate)
        act[0] = (dh * up * s * (1.0 + gate * (1.0 - s))).astype(BF16)
        act[1] = (dh * gate * s).astype(BF16)

    def rows_bwd(t):
        for c in STARTS:
            piece()
            values = []
            for n in (slice(c, c + WIDE), slice(HALF + c, HALF + c + WIDE)):
                values.append(dot_t(act[0], w_gate[n, :]) + dot_t(act[1], w_up[n, :]))
            scatter(t, c, *values)

    def hidden_fwd():
        pre[0] = dot(lhs[0], w_gate[...])
        piece()
        gate = pre[0]
        up = dot(lhs[0], w_up[...])
        act[0] = (gate * jax.nn.sigmoid(gate) * up).astype(BF16)

    def rows_fwd(t):
        for c in STARTS:
            piece()
            upper = dot(act[0], w_down[:, c : c + WIDE])
            lower = dot(act[0], w_down[:, HALF + c : HALF + c + WIDE])
            scatter(t, c, upper, lower)

    def join_home(t, cols):
        place = q + 2

        def joined(*others):
            value = ret[t, place, :, cols].astype(F32)
            for other in others:
                value = value + ret[t, other, :, cols].astype(F32)
            ret[t, place, :, cols] = value.astype(BF16)

        pl.when(q == 0)(lambda: joined(RECV + place))
        pl.when((q > 0) & (q < 3))(lambda: joined(RECV + place, RECV + place + 1))
        pl.when(q == 3)(lambda: joined(RECV + place + 1))

    def y_back_copy(t, n):
        src = ret.at[(R_B, F_B)[t], q + 2 if n == 0 else HOME]
        return remote(
            src, y_back.at[t, n], y_send_sem.at[3 + t, n], y_recv_sem.at[3 + t, n], across
        )

    def home_b(t):
        join_home((R_B, F_B)[t], pl.ds(0, HALF))
        for n in (0, 1):
            y_back_copy(t, n).start()

    def combine(t, slot_col, owner, blocks, base, out, starts):
        i, j = grid(2 * TOK, 2 * ROWS)
        within = jnp.where(j < ROWS, j, j - ROWS)
        first = (2 * owner + jnp.where(j < ROWS, half, 1 - half)) * SLOT
        slot = first + jnp.where(within < SLOT, within, within - SLOT)
        slots = jnp.concatenate([slot_col, slot_col], axis=0)
        maps = hot((slot.astype(F32) == slots) & ((within < SLOT) == (i < TOK)))
        scale = probs_col[t]
        for c in starts:
            both = [block[:, c : c + WIDE].astype(F32) for block in blocks]
            value = dot(maps, jnp.concatenate(both, axis=0).astype(BF16))
            for n, at in ((slice(c, c + WIDE), 0), (slice(HALF + c, HALF + c + WIDE), TOK)):
                added = base[:, n].astype(F32) + scale * value[at : at + TOK]
                out[:, n] = added.astype(out.dtype)

    def combine_b(t):
        for n in (0, 1):
            y_back_copy(t, n).wait_recv()
        blocks = (y_back.at[t, 0], y_back.at[t, 1])
        combine(t, slot_cols[t], 1 - plane, blocks, (g_rows, x_rows)[t], total.at[t], STARTS)

    def combine_a(t, p=None):
        side = (R_A, F_A)[t]
        join_home(side, pl.ds(0, HALF) if p is None else columns(side, p))
        starts = STARTS if p is None or PARTS[side] == 1 else (STARTS[:4], STARTS[4:])[p]
        blocks = (ret.at[side, q + 2], ret.at[side, HOME])
        combine(t, slot_cols[t], plane, blocks, total.at[t], (out_b, out_f)[t], starts)

    shift_g = remote(held_grad, g_rows, shift_send.at[0], shift_recv.at[0], before)
    shift_x = remote(held_fwd, x_rows, shift_send.at[1], shift_recv.at[1], after)

    def cross(t):
        for n in (0, 1):
            y_copy(t, n).start()

    piece()
    slot_row_b, slot_col_b, prob_b = routing(ids_b, probs_b)
    choose(0, slot_row_b)
    pl.semaphore_wait(barrier, 5)
    shift_g.start()

    piece()
    piece()
    slot_row_f, slot_col_f, prob_f = routing(ids_f, probs_f)
    slot_cols = (slot_col_b, slot_col_f)
    probs_col = (prob_b, prob_f)
    for way, ref in ((0, gathering), (1, scattering)):
        i, j = grid(2 * ALL, 2 * ALL)
        packed, whole = (j, i) if way == 0 else (i, j)
        within = lax.rem(packed, ROWS)
        goal = lax.div(packed, ROWS) * SLOT + lax.rem(within, SLOT)
        goal = goal + jnp.where(within >= SLOT, ALL, 0)
        ref[...] = hot(goal == whole)
    cross(0)

    piece()
    shift_g.wait_recv()
    choose(1, slot_row_b)
    cross(1)
    shift_x.start()

    piece()
    shift_x.wait_recv()
    choose(2, slot_row_f)
    cross(2)

    for saved_side, grad_side, back in ((S_A, G_A, R_A), (S_B, G_B, R_B)):
        piece(all_of(saved_side))
        gather(saved_side, 0)
        piece(all_of(grad_side))
        gather(grad_side, 1)
        if back == R_A:
            for copy in weight_copies:
                copy.wait()
        piece()
        hidden_bwd()
        rows_bwd(back)

    piece(all_of(X_B))
    gather(X_B, 0)
    piece()
    hidden_fwd()
    rows_fwd(F_B)

    piece(home_of(R_B, range(PARTS[R_B])))
    home_b(0)

    piece(all_of(X_A))
    gather(X_A, 0)
    piece()
    hidden_fwd()
    rows_fwd(F_A)

    piece(home_of(F_B, range(PARTS[F_B])))
    home_b(1)
    piece()
    combine_b(0)
    piece(home_of(R_A, range(PARTS[R_A])))
    combine_a(0)
    piece()
    combine_b(1)
    for p in range(PARTS[F_A]):
        piece(home_of(F_A, (p,)))
        combine_a(1, p)

    shift_g.wait_send()
    shift_x.wait_send()
    for n in (0, 1):
        for t in range(3):
            y_copy(t, n).wait_send()
        for t in range(2):
            y_back_copy(t, n).wait_send()
    for place in range(4):

        @pl.when(q == place)
        def _():
            for link in started[place]:
                for op in link[-DEPTH:]:
                    described(place, op).wait_send()


def give(from_f, from_b, to_f, to_b):
    to_f[...] = from_f[...]
    to_b[...] = from_b[...]


def on_device(
    held_fwd, ids_fwd, probs_fwd, saved_in, held_grad, ids_bwd, probs_bwd, w_gate, w_up, w_down
):
    vmem = pl.BlockSpec(memory_space=pltpu.VMEM)
    hbm = pl.BlockSpec(memory_space=pl.ANY)
    rows = jax.ShapeDtypeStruct((TOK, D), BF16)
    fwd, grad = pl.pallas_call(
        kernel,
        out_shape=(rows, rows),
        in_specs=[vmem] * 7 + [hbm] * 3,
        out_specs=(vmem, vmem),
        scratch_shapes=[
            pltpu.VMEM((D, HID), BF16),
            pltpu.VMEM((D, HID), BF16),
            pltpu.VMEM((HID, D), BF16),
            pltpu.VMEM((TOK, D), BF16),
            pltpu.VMEM((TOK, D), BF16),
            pltpu.VMEM((3, 2, ROWS, HALF), BF16),
            pltpu.VMEM((2, 2, ROWS, HALF), BF16),
            pltpu.VMEM((6, 10, ROWS, HALF), BF16),
            pltpu.VMEM((4, 19, ROWS, HALF), BF16),
            pltpu.VMEM((2, ALL, D), BF16),
            pltpu.VMEM((2, ALL, HID), BF16),
            pltpu.VMEM((2, ALL, HID), F32),
            pltpu.VMEM((2, TOK, D), F32),
            pltpu.VMEM((2 * ALL, 2 * ALL), BF16),
            pltpu.VMEM((2 * ALL, 2 * ALL), BF16),
            pltpu.SemaphoreType.DMA((3,)),
            pltpu.SemaphoreType.DMA((2,)),
            pltpu.SemaphoreType.DMA((2,)),
            pltpu.SemaphoreType.DMA((5, 2)),
            pltpu.SemaphoreType.DMA((5, 2)),
            pltpu.SemaphoreType.DMA((6, 2, STEPS)),
            pltpu.SemaphoreType.DMA((6, 10)),
            pltpu.SemaphoreType.DMA((4, 2, 2, STEPS)),
            pltpu.SemaphoreType.DMA((4, 2, 19)),
        ],
        compiler_params=pltpu.CompilerParams(
            collective_id=0, has_side_effects=True, vmem_limit_bytes=60 * 2**20
        ),
        cost_estimate=pl.CostEstimate(
            flops=7_050_000_000, bytes_accessed=12_000_000, transcendentals=300_000
        ),
        name="relay_experts",
    )(
        held_fwd[0],
        held_grad[0],
        saved_in[0],
        ids_fwd,
        probs_fwd,
        ids_bwd,
        probs_bwd,
        w_gate[0],
        w_up[0],
        w_down[0],
    )
    fwd, grad = pl.pallas_call(
        give,
        out_shape=(rows, rows),
        in_specs=[vmem, vmem],
        out_specs=(vmem, vmem),
        name="give",
    )(fwd, grad)
    return (fwd[None], grad[None])


def solution(mesh):
    return jax.shard_map(
        on_device,
        mesh=mesh,
        in_specs=(
            P("pipe", "expert", None),
            P("pipe", None),
            P("pipe", None),
            P("pipe", "expert", None),
            P("pipe", "expert", None),
            P("pipe", None),
            P("pipe", None),
            P("pipe", None, "expert"),
            P("pipe", None, "expert"),
            P("pipe", "expert", None),
        ),
        out_specs=(P("pipe", "expert", None), P("pipe", "expert", None)),
        check_vma=False,
    )
```

```python
import jax
import jax.numpy as jnp
from jax import lax
from jax.experimental import pallas as pl
from jax.experimental.pallas import tpu as pltpu
from jax.sharding import PartitionSpec as P

SLOT = 20
MESH = pl.DeviceIdType.MESH
F32 = jnp.float32
BF16 = jnp.bfloat16

D = 3584
HID = 384
TOK = 64
ROWS = 2 * SLOT
HALF = D // 2
WIDE = 256
STARTS = tuple(range(0, HALF, WIDE))
ALL = 8 * SLOT
STEPS = 6

OTHER, PASS = 8, 9
RECV, HOME, TRANSIT = 8, 17, 18
S_A, G_A, S_B, G_B, X_B, X_A = range(6)
R_A, R_B, F_B, F_A = range(4)
PARTS = (2, 2, 2, 2)
DEPTH = 3
RAWS = (0, 1, 2)
TENSOR = (0, 1, 0, 1, 2, 2)

ORDER = (
    (
        (),
        (),
        ((0, 0, 0), (0, 1, 0)),
        ((0, 0, 1), (2, 0, 0), (2, 1, 0)),
        (),
        ((1, 0, 0), (1, 1, 0)),
        ((0, 1, 1), (2, 0, 1), (3, 0, 0), (1, 0, 1), (3, 1, 0)),
        ((0, 0, 2), (5, 1, 0), (3, 0, 1)),
        ((1, 1, 1), (2, 1, 1), (5, 0, 0), (4, 0, 0), (4, 1, 0), (1, 0, 2), (2, 0, 2), (3, 1, 1), (4, 0, 1), (3, 0, 2), (5, 0, 1)),
        (),
        (),
        (),
        (),
        (),
        (),
        (),
        (),
        ((6, 1, 0), (6, 1, 1)),
        (),
        (),
        (),
        ((7, 1, 0), (5, 1, 1), (7, 1, 1)),
        ((6, 1, 2), (7, 1, 2), (5, 0, 2), (6, 1, 3), (4, 1, 1), (7, 1, 3), (6, 1, 4), (4, 0, 2)),
        (),
        ((7, 1, 4),),
        (),
        (),
        (),
        (),
        (),
        ((8, 1, 0),),
        ((8, 1, 1),),
        (),
        ((9, 1, 0), (9, 1, 1), (8, 1, 2), (6, 0, 3), (9, 1, 2), (7, 0, 3), (8, 1, 3), (9, 1, 3)),
        (),
        ((8, 1, 4),),
        ((8, 0, 3), (9, 1, 4)),
        (),
        ((8, 0, 4),),
        (),
        ((10, 1, 0),),
        (),
        ((9, 0, 3),),
        ((11, 1, 0), (9, 0, 4), (8, 1, 5), (10, 1, 1)),
        ((9, 1, 5), (11, 1, 1), (10, 1, 2), (11, 1, 2), (10, 1, 3), (11, 1, 3), (6, 1, 5), (7, 1, 5)),
        (),
        ((10, 1, 4),),
        ((6, 0, 4), (11, 1, 4)),
        ((7, 0, 4),),
        (),
        (),
        ((12, 1, 0),),
        (),
        ((10, 0, 3),),
        ((13, 1, 0), (11, 0, 3), (12, 1, 1), (13, 1, 1), (10, 1, 5), (10, 0, 4), (11, 1, 5), (11, 0, 4), (12, 1, 2), (13, 1, 2)),
        (),
        ((12, 0, 3), (12, 1, 3), (13, 1, 3)),
        ((13, 0, 3), (12, 0, 4), (12, 1, 4), (13, 1, 4), (13, 0, 4), (12, 1, 5)),
        ((13, 1, 5),),
        (),
    ),
    (
        (),
        ((14, 1, 0),),
        ((0, 0, 0),),
        ((0, 0, 1), (0, 1, 2), (2, 0, 0), (0, 0, 2)),
        (),
        ((15, 1, 0), (1, 0, 0)),
        ((0, 1, 3), (2, 0, 1), (1, 0, 1)),
        ((2, 0, 2),),
        ((0, 1, 4), (3, 0, 0), (1, 1, 2), (1, 0, 2), (1, 1, 3), (0, 0, 3), (16, 1, 0), (3, 0, 1), (1, 1, 4), (3, 0, 2)),
        ((4, 0, 0), (1, 0, 3), (2, 0, 3), (0, 1, 5), (4, 0, 1), (2, 1, 2)),
        (),
        (),
        ((1, 1, 5), (3, 0, 3)),
        (),
        (),
        (),
        (),
        ((4, 0, 2),),
        ((2, 1, 3),),
        (),
        (),
        (),
        ((5, 0, 0), (2, 1, 4)),
        (),
        (),
        ((2, 1, 5), (5, 0, 1)),
        (),
        (),
        (),
        (),
        ((5, 0, 2),),
        ((3, 1, 2),),
        (),
        ((3, 1, 3), (6, 1, 1), (6, 1, 2), (3, 1, 4), (7, 1, 1), (3, 1, 5), (7, 1, 2), (6, 1, 3), (7, 1, 3), (4, 1, 2), (5, 0, 3), (4, 1, 3), (6, 1, 4), (7, 1, 4), (4, 1, 4), (6, 0, 2), (4, 0, 3), (7, 0, 2), (8, 1, 1)),
        ((4, 1, 5), (8, 1, 2)),
        ((9, 1, 1), (8, 0, 2)),
        ((9, 1, 2),),
        (),
        (),
        ((8, 0, 3), (8, 1, 3)),
        (),
        (),
        ((9, 1, 3), (9, 0, 2)),
        ((8, 1, 4), (9, 0, 3), (9, 1, 4), (8, 0, 4), (9, 0, 4), (5, 1, 2), (5, 1, 3), (10, 1, 1), (11, 1, 1), (5, 1, 4), (10, 1, 2), (5, 1, 5)),
        (),
        ((11, 1, 2),),
        (),
        ((6, 0, 3), (10, 1, 3)),
        (),
        ((11, 1, 3),),
        (),
        (),
        (),
        (),
        ((7, 0, 3), (10, 1, 4), (11, 1, 4), (10, 0, 2), (11, 0, 2), (6, 0, 4), (7, 0, 4), (10, 0, 3), (11, 0, 3), (12, 1, 1), (13, 1, 1), (10, 0, 4), (11, 0, 4), (12, 1, 2), (13, 1, 2), (12, 0, 2), (13, 0, 2)),
        ((12, 0, 3),),
        ((12, 1, 3), (13, 0, 3)),
        ((13, 1, 3), (12, 1, 4), (12, 0, 4), (13, 1, 4), (13, 0, 4)),
        (),
        (),
    ),
    (
        (),
        ((14, 0, 0),),
        ((0, 1, 0),),
        ((0, 1, 1), (0, 0, 2), (2, 1, 0), (0, 1, 2)),
        (),
        ((15, 0, 0), (1, 1, 0)),
        ((0, 0, 3), (2, 1, 1), (1, 1, 1)),
        ((2, 1, 2),),
        ((0, 0, 4), (3, 1, 0), (1, 0, 2), (1, 1, 2), (1, 0, 3), (0, 1, 3), (16, 0, 0), (3, 1, 1), (1, 0, 4), (3, 1, 2)),
        ((4, 1, 0), (1, 1, 3), (2, 1, 3), (0, 0, 5), (4, 1, 1), (2, 0, 2)),
        (),
        (),
        ((3, 1, 3), (1, 0, 5)),
        (),
        (),
        (),
        (),
        ((4, 1, 2),),
        ((2, 0, 3),),
        (),
        (),
        (),
        ((5, 1, 0), (2, 0, 4)),
        (),
        (),
        ((5, 1, 1), (2, 0, 5)),
        (),
        (),
        (),
        (),
        ((5, 1, 2),),
        ((3, 0, 2),),
        (),
        ((3, 0, 3), (6, 0, 1), (6, 0, 2), (3, 0, 4), (7, 0, 1), (3, 0, 5), (7, 0, 2), (6, 0, 3), (7, 0, 3), (4, 0, 2), (5, 1, 3), (4, 0, 3), (6, 0, 4), (7, 0, 4), (4, 0, 4), (6, 1, 2), (4, 1, 3), (7, 1, 2), (8, 0, 1)),
        ((4, 0, 5), (8, 0, 2)),
        ((9, 0, 1), (8, 1, 2)),
        ((9, 0, 2),),
        (),
        (),
        ((8, 1, 3), (8, 0, 3)),
        (),
        (),
        ((9, 0, 3), (9, 1, 2)),
        ((8, 0, 4), (9, 1, 3), (9, 0, 4), (8, 1, 4), (9, 1, 4), (5, 0, 2), (5, 0, 3), (10, 0, 1), (11, 0, 1), (5, 0, 4), (10, 0, 2), (5, 0, 5)),
        (),
        ((11, 0, 2),),
        (),
        ((6, 1, 3), (10, 0, 3)),
        (),
        ((11, 0, 3),),
        (),
        (),
        (),
        (),
        ((7, 1, 3), (10, 0, 4), (11, 0, 4), (10, 1, 2), (11, 1, 2), (6, 1, 4), (7, 1, 4), (10, 1, 3), (11, 1, 3), (12, 0, 1), (13, 0, 1), (10, 1, 4), (11, 1, 4), (12, 0, 2), (13, 0, 2), (12, 1, 2), (13, 1, 2)),
        ((12, 1, 3),),
        ((12, 0, 3), (13, 1, 3)),
        ((13, 0, 3), (12, 0, 4), (12, 1, 4), (13, 0, 4), (13, 1, 4)),
        (),
        (),
    ),
    (
        (),
        (),
        ((0, 0, 0), (0, 1, 0)),
        ((0, 1, 1), (2, 1, 0), (2, 0, 0)),
        (),
        ((1, 0, 0), (1, 1, 0)),
        ((0, 0, 1), (2, 1, 1), (3, 1, 0), (1, 1, 1), (3, 0, 0)),
        ((0, 1, 2), (5, 0, 0), (3, 1, 1)),
        ((1, 0, 1), (2, 0, 1), (5, 1, 0), (4, 1, 0), (4, 0, 0), (1, 1, 2), (2, 1, 2), (3, 0, 1), (4, 1, 1), (3, 1, 2), (5, 1, 1)),
        (),
        (),
        (),
        (),
        (),
        (),
        (),
        (),
        ((6, 0, 0), (6, 0, 1)),
        (),
        (),
        (),
        ((7, 0, 0), (5, 0, 1), (7, 0, 1)),
        ((6, 0, 2), (7, 0, 2), (5, 1, 2), (6, 0, 3), (4, 0, 1), (7, 0, 3), (6, 0, 4), (4, 1, 2)),
        (),
        ((7, 0, 4),),
        (),
        (),
        (),
        (),
        (),
        ((8, 0, 0),),
        ((8, 0, 1),),
        (),
        ((9, 0, 0), (9, 0, 1), (8, 0, 2), (6, 1, 3), (9, 0, 2), (7, 1, 3), (8, 0, 3), (9, 0, 3)),
        (),
        ((8, 0, 4),),
        ((8, 1, 3), (9, 0, 4)),
        (),
        ((8, 1, 4),),
        (),
        ((10, 0, 0),),
        (),
        ((9, 1, 3),),
        ((11, 0, 0), (9, 1, 4), (8, 0, 5), (10, 0, 1)),
        ((9, 0, 5), (11, 0, 1), (10, 0, 2), (11, 0, 2), (10, 0, 3), (11, 0, 3), (6, 0, 5), (7, 0, 5)),
        (),
        ((10, 0, 4),),
        ((6, 1, 4), (11, 0, 4)),
        ((7, 1, 4),),
        (),
        (),
        ((12, 0, 0),),
        (),
        ((10, 1, 3),),
        ((13, 0, 0), (11, 1, 3), (12, 0, 1), (13, 0, 1), (10, 0, 5), (10, 1, 4), (11, 0, 5), (11, 1, 4), (12, 0, 2), (13, 0, 2)),
        (),
        ((12, 0, 3), (12, 1, 3), (13, 0, 3)),
        ((13, 1, 3), (12, 0, 4), (12, 1, 4), (13, 0, 4), (13, 1, 4), (12, 0, 5)),
        ((13, 0, 5),),
        (),
    ),
)


def mirrored(index):
    return 7 - index if index < 8 else index


def out_plan(right, k):
    plan = []
    for q in range(4):
        place = q if right else 3 - q
        active, src, dst = False, 0, 0
        if place < 2 and k < place + 3:
            active, src = True, place - k + 2
            dst = src
        elif place == 2:
            active = True
            src, dst = (OTHER, PASS) if k == 0 else (5 - k, 5 - k)
        elif place == 3 and k < 2:
            active, src, dst = True, OTHER + k, 1 - k
        if not right:
            src, dst = mirrored(src), mirrored(dst)
        plan.append((active, src, dst))
    return plan


def back_plan(left, k):
    plan = []
    for q in range(4):
        place = q if left else 3 - q
        active, src, dst, added = False, 0, 0, -1
        if 3 - place <= k <= 4:
            index = k - 3 + place
            active = True
            src = index if left else 7 - index
            slot = RECV + index if left else 16 - index
            dst = slot if place > 0 else TRANSIT - index
            added = slot if place < 3 else -1
        elif place == 3 and k == 5:
            active, src, dst = True, TRANSIT, HOME
        plan.append((active, src, dst, added))
    return plan


def kernel(
    held_fwd,
    held_grad,
    saved,
    ids_f,
    probs_f,
    ids_b,
    probs_b,
    w_gate_hbm,
    w_up_hbm,
    w_down_hbm,
    out_f,
    out_b,
    w_gate,
    w_up,
    w_down,
    x_rows,
    g_rows,
    y_out,
    y_back,
    raw,
    edge_out,
    blk,
    ret,
    lhs,
    act,
    pre,
    total,
    gathering,
    scattering,
    w_sem,
    shift_send,
    shift_recv,
    y_send_sem,
    y_recv_sem,
    raw_send_sem,
    raw_recv_sem,
    edge_send_sem,
    edge_recv_sem,
    out_send_sem,
    out_recv_sem,
    back_send_sem,
    back_recv_sem,
):
    pipe = lax.axis_index("pipe")
    position = lax.axis_index("expert")
    plane = position // 8
    z = position % 8
    half = z // 4
    q = z % 4
    right = (pipe, plane * 8 + (z + 1) % 8)
    left = (pipe, plane * 8 + (z + 7) % 8)
    across = (pipe, (1 - plane) * 8 + z)
    after = ((pipe + 1) % 16, position)
    before = ((pipe + 15) % 16, position)

    barrier = pltpu.get_barrier_semaphore()
    for device in (right, left, across, after, before):
        pl.semaphore_signal(barrier, inc=1, device_id=device, device_id_type=MESH)

    weight_copies = [
        pltpu.make_async_copy(w_gate_hbm, w_gate, w_sem.at[0]),
        pltpu.make_async_copy(w_up_hbm, w_up, w_sem.at[1]),
        pltpu.make_async_copy(w_down_hbm, w_down, w_sem.at[2]),
    ]
    for copy in weight_copies:
        copy.start()

    def remote(src, dst, send_sem, recv_sem, device):
        return pltpu.make_async_remote_copy(
            src_ref=src,
            dst_ref=dst,
            send_sem=send_sem,
            recv_sem=recv_sem,
            device_id=device,
            device_id_type=MESH,
        )

    def grid(rows, cols):
        return (
            lax.broadcasted_iota(jnp.int32, (rows, cols), 0),
            lax.broadcasted_iota(jnp.int32, (rows, cols), 1),
        )

    def hot(mask):
        return jnp.where(mask, jnp.float32(1), jnp.float32(0)).astype(BF16)

    def dot(a, b):
        return jnp.dot(a, b, preferred_element_type=F32)

    def dot_t(a, b):
        return lax.dot_general(a, b, (((1,), (1,)), ((), ())), preferred_element_type=F32)

    def part_of(ref, position):
        base = pl.multiple_of((position // 2) * 128, 128)
        both = ref[:, pl.ds(base, 128)].astype(F32)
        return jnp.where(position % 2 == 0, both[:, :TOK], both[:, TOK:])

    def upright(row):
        i, j = grid(TOK, TOK)
        return jnp.sum(jnp.where(i == j, row, jnp.float32(0)), axis=1, keepdims=True)

    def routing(ids_ref, probs_ref, position):
        row = part_of(ids_ref, position)
        col = upright(row)
        i, j = grid(TOK, TOK)
        one, none = jnp.float32(1), jnp.float32(0)
        rank_row = jnp.sum(jnp.where((row == col) & (i < j), one, none), axis=0, keepdims=True)
        rank_col = jnp.sum(jnp.where((row == col) & (j < i), one, none), axis=1, keepdims=True)
        return row * SLOT + rank_row, col * SLOT + rank_col, upright(part_of(probs_ref, position))

    sources = (saved, g_rows, x_rows)

    def choose(rows, slot_row, blocks):
        experts = [2 * side + line for side in (plane, 1 - plane) for line in (half, 1 - half)]
        i, j = grid(ROWS, 2 * TOK)
        slots = jnp.concatenate([slot_row, slot_row], axis=1)
        slots = jnp.where((i < SLOT) == (j < TOK), slots, jnp.float32(-1))
        offset = jnp.where(i < SLOT, i, i - SLOT)
        maps = [
            jnp.where((offset + expert * SLOT).astype(F32) == slots, jnp.float32(1), jnp.float32(0))
            for expert in experts
        ]
        maps = jnp.concatenate(maps, axis=0).astype(BF16)
        for c in STARTS:
            upper = rows[:, c : c + WIDE]
            lower = rows[:, HALF + c : HALF + c + WIDE]
            value = dot(maps, jnp.concatenate([upper, lower], axis=0))
            for n in range(4):
                blocks[n][:, c : c + WIDE] = value[n * ROWS : (n + 1) * ROWS].astype(BF16)

    on_edge = (q == 0) | (q == 3)
    near = jnp.where(q == 3, 4, 3)

    def choose_own(t, slot_row):
        side = (S_A, G_A, X_A)[t]
        blocks = (blk.at[side, q + 2], blk.at[side, OTHER], y_out.at[t, 0], y_out.at[t, 1])
        choose(sources[t], slot_row, blocks)

    def choose_near(t, slot_row):
        side = (S_A, G_A, X_A)[t]
        blocks = (blk.at[side, near], blk.at[side, PASS], edge_out.at[t, 0], edge_out.at[t, 1])
        choose(raw.at[t], slot_row, blocks)

    def edge_copy(t, n):
        side = (S_B, G_B, X_B)[t]
        place = near if n == 0 else PASS
        return remote(
            edge_out.at[t, n],
            blk.at[side, place],
            edge_send_sem.at[t, n],
            edge_recv_sem.at[t, n],
            across,
        )

    def raw_copy(t, way):
        return remote(
            sources[t], raw.at[t], raw_send_sem.at[t], raw_recv_sem.at[t], right if way == 0 else left
        )

    def y_copy(t, n):
        side = (S_B, G_B, X_B)[t]
        place = q + 2 if n == 0 else OTHER
        return remote(
            y_out.at[t, n], blk.at[side, place], y_send_sem.at[t, n], y_recv_sem.at[t, n], across
        )

    def columns(t, p):
        if PARTS[t] == 1:
            return pl.ds(0, HALF)
        return pl.ds(0, 4 * WIDE) if p == 0 else pl.ds(4 * WIDE, 3 * WIDE)

    def out_copy(t, way, k, src, dst):
        return remote(
            blk.at[t, src],
            blk.at[t, dst],
            out_send_sem.at[t, way, k],
            out_recv_sem.at[t, dst],
            right if way == 0 else left,
        )

    def back_copy(t, p, way, k, src, dst):
        return remote(
            ret.at[t, src, :, columns(t, p)],
            ret.at[t, dst, :, columns(t, p)],
            back_send_sem.at[t, p, way, k],
            back_recv_sem.at[t, p, dst],
            left if way == 0 else right,
        )

    arrived = [set() for _ in range(4)]
    started = [([], []) for _ in range(4)]

    def need(place, key):
        if key in arrived[place]:
            return
        arrived[place].add(key)
        picked = key[0] == "out" and place in (0, 3) and TENSOR[key[1]] in RAWS
        if key[0] == "raw":
            raw_copy(key[1], 0).wait_recv()
        elif picked and key[2] in (4 if place == 3 else 3, PASS):
            if key[1] in (S_B, G_B, X_B):
                edge_copy(TENSOR[key[1]], 0 if key[2] < 8 else 1).wait_recv()
        elif key[0] == "out":
            out_copy(key[1], 0, 0, key[2], key[2]).wait_recv()
        elif key[0] == "back":
            back_copy(key[1], key[2], 0, 0, key[3], key[3]).wait_recv()
        elif key[1] in (S_B, G_B, X_B):
            y_copy(TENSOR[key[1]], key[2]).wait_recv()

    def described(place, op):
        stream, way, k = op
        if stream >= 14:
            return raw_copy(stream - 14, way)
        if stream < 6:
            _, src, dst = out_plan(way == 0, k)[place]
            return out_copy(stream, way, k, src, dst)
        t, p = (stream - 6) // 2, (stream - 6) % 2
        _, src, dst, _ = back_plan(way == 0, k)[place]
        return back_copy(t, p, way, k, src, dst)

    def start(place, op):
        stream, way, k = op
        if stream < 6:
            _, src, _ = out_plan(way == 0, k)[place]
            if src == place + 2:
                need(place, ("own", stream, 0))
            elif src == OTHER:
                need(place, ("own", stream, 1))
            else:
                need(place, ("out", stream, src))
        elif stream < 14:
            t, p = (stream - 6) // 2, (stream - 6) % 2
            _, src, _, added = back_plan(way == 0, k)[place]
            if src == TRANSIT:
                need(place, ("back", t, p, TRANSIT))
            if added >= 0:
                need(place, ("back", t, p, added))
                cols = columns(t, p)
                joined = ret[t, src, :, cols].astype(F32) + ret[t, added, :, cols].astype(F32)
                ret[t, src, :, cols] = joined.astype(BF16)
        link = started[place][(way == 0) == (stream < 6 or stream >= 14)]
        if len(link) >= DEPTH:
            described(place, link[-DEPTH]).wait_send()
        link.append(op)
        described(place, op).start()

    def all_of(*sides):
        def keys(place):
            found = []
            for side in sides:
                found.append(("own", side, 0))
                found += [("out", side, i) for i in range(8) if i != place + 2]
            return found

        return keys

    def home_of(t, parts):
        def keys(place):
            found = []
            for p in parts:
                found.append(("back", t, p, HOME))
                if place < 3:
                    found.append(("back", t, p, RECV + place + 2))
                if place > 0:
                    found.append(("back", t, p, RECV + place + 3))
            return found

        return keys

    def nothing(place):
        return []

    count = [0]

    def piece(keys=nothing):
        number = count[0]
        count[0] += 1
        for place in range(4):
            ops = ORDER[place][number]
            if ops or any(key not in arrived[place] for key in keys(place)):

                @pl.when(q == place)
                def _():
                    for op in ops:
                        start(place, op)
                    for key in keys(place):
                        need(place, key)

    def gather(t, to):
        for c in STARTS:
            rows = [blk[t, i, :, c : c + WIDE].astype(F32) for i in range(8)]
            value = dot(gathering[...], jnp.concatenate(rows, axis=0).astype(BF16)).astype(BF16)
            lhs[to, :, c : c + WIDE] = value[:ALL]
            lhs[to, :, HALF + c : HALF + c + WIDE] = value[ALL:]

    def scatter(t, c, upper, lower):
        both = jnp.concatenate([upper, lower], axis=0).astype(BF16)
        value = dot(scattering[...], both)
        for i in range(8):
            ret[t, i, :, c : c + WIDE] = value[i * ROWS : (i + 1) * ROWS].astype(BF16)

    def hidden_bwd():
        pre[0] = dot(lhs[0], w_gate[...])
        piece()
        pre[1] = dot(lhs[0], w_up[...])
        piece()
        dh = dot_t(lhs[1], w_down[...])
        gate, up = pre[0], pre[1]
        s = jax.nn.sigmoid(gate)
        act[0] = (dh * up * s * (1.0 + gate * (1.0 - s))).astype(BF16)
        act[1] = (dh * gate * s).astype(BF16)

    def rows_bwd(t):
        for c in STARTS:
            piece()
            values = []
            for n in (slice(c, c + WIDE), slice(HALF + c, HALF + c + WIDE)):
                values.append(dot_t(act[0], w_gate[n, :]) + dot_t(act[1], w_up[n, :]))
            scatter(t, c, *values)

    def hidden_fwd():
        pre[0] = dot(lhs[0], w_gate[...])
        piece()
        gate = pre[0]
        up = dot(lhs[0], w_up[...])
        act[0] = (gate * jax.nn.sigmoid(gate) * up).astype(BF16)

    def rows_fwd(t):
        for c in STARTS:
            piece()
            upper = dot(act[0], w_down[:, c : c + WIDE])
            lower = dot(act[0], w_down[:, HALF + c : HALF + c + WIDE])
            scatter(t, c, upper, lower)

    def join_home(t, cols):
        place = q + 2

        def joined(*others):
            value = ret[t, place, :, cols].astype(F32)
            for other in others:
                value = value + ret[t, other, :, cols].astype(F32)
            ret[t, place, :, cols] = value.astype(BF16)

        pl.when(q == 0)(lambda: joined(RECV + place))
        pl.when((q > 0) & (q < 3))(lambda: joined(RECV + place, RECV + place + 1))
        pl.when(q == 3)(lambda: joined(RECV + place + 1))

    def y_back_copy(t, n):
        src = ret.at[(R_B, F_B)[t], q + 2 if n == 0 else HOME]
        return remote(
            src, y_back.at[t, n], y_send_sem.at[3 + t, n], y_recv_sem.at[3 + t, n], across
        )

    def home_b(t):
        join_home((R_B, F_B)[t], pl.ds(0, HALF))
        for n in (0, 1):
            y_back_copy(t, n).start()

    def combine(t, slot_col, owner, blocks, base, out, starts):
        i, j = grid(2 * TOK, 2 * ROWS)
        within = jnp.where(j < ROWS, j, j - ROWS)
        first = (2 * owner + jnp.where(j < ROWS, half, 1 - half)) * SLOT
        slot = first + jnp.where(within < SLOT, within, within - SLOT)
        slots = jnp.concatenate([slot_col, slot_col], axis=0)
        maps = hot((slot.astype(F32) == slots) & ((within < SLOT) == (i < TOK)))
        scale = probs_col[t]
        for c in starts:
            both = [block[:, c : c + WIDE].astype(F32) for block in blocks]
            value = dot(maps, jnp.concatenate(both, axis=0).astype(BF16))
            for n, at in ((slice(c, c + WIDE), 0), (slice(HALF + c, HALF + c + WIDE), TOK)):
                added = base[:, n].astype(F32) + scale * value[at : at + TOK]
                out[:, n] = added.astype(out.dtype)

    def combine_b(t):
        for n in (0, 1):
            y_back_copy(t, n).wait_recv()
        blocks = (y_back.at[t, 0], y_back.at[t, 1])
        combine(t, slot_cols[t], 1 - plane, blocks, (g_rows, x_rows)[t], total.at[t], STARTS)

    def combine_a(t, p=None):
        side = (R_A, F_A)[t]
        join_home(side, pl.ds(0, HALF) if p is None else columns(side, p))
        starts = STARTS if p is None or PARTS[side] == 1 else (STARTS[:4], STARTS[4:])[p]
        blocks = (ret.at[side, q + 2], ret.at[side, HOME])
        combine(t, slot_cols[t], plane, blocks, total.at[t], (out_b, out_f)[t], starts)

    shift_g = remote(held_grad, g_rows, shift_send.at[0], shift_recv.at[0], before)
    shift_x = remote(held_fwd, x_rows, shift_send.at[1], shift_recv.at[1], after)

    def crossing(t, act):
        act(y_copy(t, 0))
        if t in RAWS:
            pl.when(on_edge)(lambda: act(y_copy(t, 1)))
        else:
            act(y_copy(t, 1))

    def cross(t):
        crossing(t, lambda copy: copy.start())

    def raw_of(t):
        return lambda place: [("raw", t)] if place in (0, 3) else []

    def pick_near(t):
        if t not in RAWS:
            return
        piece(raw_of(t))

        @pl.when(on_edge)
        def _():
            choose_near(t, (near_b, near_b, near_f)[t])
            for n in (0, 1):
                edge_copy(t, n).start()

    piece()
    slot_row_b, slot_col_b, prob_b = routing(ids_b, probs_b, position)
    choose_own(0, slot_row_b)
    pl.semaphore_wait(barrier, 5)
    shift_g.start()

    piece()
    piece()
    slot_row_f, slot_col_f, prob_f = routing(ids_f, probs_f, position)
    neighbour = position + jnp.where(q == 0, 1, 0) - jnp.where(q == 3, 1, 0)
    near_b = routing(ids_b, probs_b, neighbour)[0]
    near_f = routing(ids_f, probs_f, neighbour)[0]
    slot_cols = (slot_col_b, slot_col_f)
    probs_col = (prob_b, prob_f)
    for way, ref in ((0, gathering), (1, scattering)):
        i, j = grid(2 * ALL, 2 * ALL)
        packed, whole = (j, i) if way == 0 else (i, j)
        within = lax.rem(packed, ROWS)
        goal = lax.div(packed, ROWS) * SLOT + lax.rem(within, SLOT)
        goal = goal + jnp.where(within >= SLOT, ALL, 0)
        ref[...] = hot(goal == whole)
    cross(0)

    piece()
    shift_g.wait_recv()

    piece()
    choose_own(1, slot_row_b)
    cross(1)
    shift_x.start()
    pick_near(0)

    piece()
    shift_x.wait_recv()
    choose_own(2, slot_row_f)
    cross(2)
    pick_near(1)

    for saved_side, grad_side, back in ((S_A, G_A, R_A), (S_B, G_B, R_B)):
        piece(all_of(saved_side))
        gather(saved_side, 0)
        piece(all_of(grad_side))
        gather(grad_side, 1)
        if back == R_A:
            for copy in weight_copies:
                copy.wait()
        piece()
        hidden_bwd()
        rows_bwd(back)
        if back == R_A:
            pick_near(2)

    piece(all_of(X_B))
    gather(X_B, 0)
    piece()
    hidden_fwd()
    rows_fwd(F_B)

    piece(home_of(R_B, range(PARTS[R_B])))
    home_b(0)

    piece(all_of(X_A))
    gather(X_A, 0)
    piece()
    hidden_fwd()
    rows_fwd(F_A)

    piece(home_of(F_B, range(PARTS[F_B])))
    home_b(1)
    piece()
    combine_b(0)
    piece(home_of(R_A, range(PARTS[R_A])))
    combine_a(0)
    piece()
    combine_b(1)
    for p in range(PARTS[F_A]):
        piece(home_of(F_A, (p,)))
        combine_a(1, p)

    shift_g.wait_send()
    shift_x.wait_send()
    for t in range(3):
        crossing(t, lambda copy: copy.wait_send())
    for t in range(2):
        for n in (0, 1):
            y_back_copy(t, n).wait_send()
    for t in RAWS:
        for n in (0, 1):
            pl.when(on_edge)(lambda: edge_copy(t, n).wait_send())
    for place in range(4):

        @pl.when(q == place)
        def _():
            for link in started[place]:
                for op in link[-DEPTH:]:
                    described(place, op).wait_send()


def give(from_f, from_b, to_f, to_b):
    to_f[...] = from_f[...]
    to_b[...] = from_b[...]


def on_device(
    held_fwd, ids_fwd, probs_fwd, saved_in, held_grad, ids_bwd, probs_bwd, w_gate, w_up, w_down
):
    vmem = pl.BlockSpec(memory_space=pltpu.VMEM)
    hbm = pl.BlockSpec(memory_space=pl.ANY)
    rows = jax.ShapeDtypeStruct((TOK, D), BF16)
    fwd, grad = pl.pallas_call(
        kernel,
        out_shape=(rows, rows),
        in_specs=[vmem] * 7 + [hbm] * 3,
        out_specs=(vmem, vmem),
        scratch_shapes=[
            pltpu.VMEM((D, HID), BF16),
            pltpu.VMEM((D, HID), BF16),
            pltpu.VMEM((HID, D), BF16),
            pltpu.VMEM((TOK, D), BF16),
            pltpu.VMEM((TOK, D), BF16),
            pltpu.VMEM((3, 2, ROWS, HALF), BF16),
            pltpu.VMEM((2, 2, ROWS, HALF), BF16),
            pltpu.VMEM((3, TOK, D), BF16),
            pltpu.VMEM((3, 2, ROWS, HALF), BF16),
            pltpu.VMEM((6, 10, ROWS, HALF), BF16),
            pltpu.VMEM((4, 19, ROWS, HALF), BF16),
            pltpu.VMEM((2, ALL, D), BF16),
            pltpu.VMEM((2, ALL, HID), BF16),
            pltpu.VMEM((2, ALL, HID), F32),
            pltpu.VMEM((2, TOK, D), F32),
            pltpu.VMEM((2 * ALL, 2 * ALL), BF16),
            pltpu.VMEM((2 * ALL, 2 * ALL), BF16),
            pltpu.SemaphoreType.DMA((3,)),
            pltpu.SemaphoreType.DMA((2,)),
            pltpu.SemaphoreType.DMA((2,)),
            pltpu.SemaphoreType.DMA((5, 2)),
            pltpu.SemaphoreType.DMA((5, 2)),
            pltpu.SemaphoreType.DMA((3,)),
            pltpu.SemaphoreType.DMA((3,)),
            pltpu.SemaphoreType.DMA((3, 2)),
            pltpu.SemaphoreType.DMA((3, 2)),
            pltpu.SemaphoreType.DMA((6, 2, STEPS)),
            pltpu.SemaphoreType.DMA((6, 10)),
            pltpu.SemaphoreType.DMA((4, 2, 2, STEPS)),
            pltpu.SemaphoreType.DMA((4, 2, 19)),
        ],
        compiler_params=pltpu.CompilerParams(
            collective_id=0, has_side_effects=True, vmem_limit_bytes=60 * 2**20
        ),
        cost_estimate=pl.CostEstimate(
            flops=7_050_000_000, bytes_accessed=12_000_000, transcendentals=300_000
        ),
        name="relay_experts",
    )(
        held_fwd[0],
        held_grad[0],
        saved_in[0],
        ids_fwd,
        probs_fwd,
        ids_bwd,
        probs_bwd,
        w_gate[0],
        w_up[0],
        w_down[0],
    )
    fwd, grad = pl.pallas_call(
        give,
        out_shape=(rows, rows),
        in_specs=[vmem, vmem],
        out_specs=(vmem, vmem),
        name="give",
    )(fwd, grad)
    return (fwd[None], grad[None])


def solution(mesh):
    return jax.shard_map(
        on_device,
        mesh=mesh,
        in_specs=(
            P("pipe", "expert", None),
            P("pipe", None),
            P("pipe", None),
            P("pipe", "expert", None),
            P("pipe", "expert", None),
            P("pipe", None),
            P("pipe", None),
            P("pipe", None, "expert"),
            P("pipe", None, "expert"),
            P("pipe", "expert", None),
        ),
        out_specs=(P("pipe", "expert", None), P("pipe", "expert", None)),
        check_vma=False,
    )
```

```python
import jax
import jax.numpy as jnp
from jax import lax
from jax.experimental import pallas as pl
from jax.experimental.pallas import tpu as pltpu
from jax.sharding import PartitionSpec as P

SLOT = 20
MESH = pl.DeviceIdType.MESH
F32 = jnp.float32
BF16 = jnp.bfloat16

D = 3584
HID = 384
TOK = 64
TOKENS = 1024
ROWS = 2 * SLOT
HALF = D // 2
WIDE = 256
STARTS = tuple(range(0, HALF, WIDE))
ALL = 8 * SLOT
STEPS = 6

OTHER, PASS = 8, 9
RECV, HOME, TRANSIT = 8, 17, 18
S_A, G_A, S_B, G_B, X_B, X_A = range(6)
R_A, R_B, F_B, F_A = range(4)
PARTS = (1, 1, 2, 2)
DEPTH = 3
RAWS = (0, 1)
TENSOR = (0, 1, 0, 1, 2, 2)

ORDER = (
    (
        (),
        (),
        ((0, 0, 0), (0, 1, 0)),
        ((0, 0, 1), (2, 0, 0)),
        (),
        ((1, 0, 0), (1, 1, 0)),
        ((2, 1, 0), (0, 1, 1), (3, 0, 0), (1, 0, 1), (3, 1, 0), (2, 0, 1), (0, 0, 2)),
        ((1, 1, 1), (2, 1, 1), (3, 0, 1)),
        ((5, 0, 0), (5, 1, 0), (1, 0, 2), (3, 1, 1), (2, 0, 2), (4, 0, 0), (4, 1, 0), (3, 0, 2), (4, 0, 1), (5, 0, 1)),
        (),
        (),
        (),
        (),
        (),
        (),
        (),
        (),
        (),
        (),
        (),
        ((6, 1, 0), (6, 1, 1)),
        ((6, 1, 2), (4, 1, 1), (6, 1, 3)),
        ((6, 1, 4),),
        (),
        (),
        (),
        ((4, 0, 2),),
        (),
        (),
        (),
        (),
        (),
        ((8, 1, 0), (8, 1, 1), (8, 1, 2), (5, 1, 1), (8, 1, 3), (8, 1, 4), (5, 0, 2)),
        (),
        (),
        (),
        (),
        (),
        ((8, 0, 3),),
        ((10, 1, 0), (10, 1, 1)),
        (),
        (),
        ((8, 0, 4), (11, 1, 0), (11, 1, 1), (8, 1, 5), (10, 1, 2)),
        ((11, 1, 2), (10, 1, 3), (11, 1, 3), (10, 0, 3), (11, 0, 3), (10, 1, 4), (11, 1, 4)),
        ((10, 1, 5),),
        ((11, 1, 5), (10, 0, 4)),
        (),
        (),
        (),
        (),
        ((12, 1, 0),),
        ((12, 1, 1),),
        ((6, 0, 3),),
        ((11, 0, 4), (13, 1, 0), (13, 1, 1), (12, 1, 2), (6, 1, 5), (6, 0, 4)),
        ((13, 1, 2),),
        ((12, 1, 3),),
        ((12, 0, 3), (13, 1, 3), (13, 0, 3), (12, 1, 4), (13, 1, 4), (12, 0, 4)),
        ((13, 0, 4), (12, 1, 5), (13, 1, 5)),
        (),
    ),
    (
        (),
        ((14, 1, 0),),
        ((0, 0, 0),),
        ((0, 0, 1), (0, 1, 2), (2, 0, 0)),
        (),
        ((1, 0, 0), (15, 1, 0)),
        (),
        ((0, 1, 3), (0, 0, 2), (2, 0, 1), (1, 0, 1)),
        ((3, 0, 0), (1, 1, 2), (1, 0, 2), (2, 1, 2), (2, 0, 2), (1, 1, 3), (0, 0, 3), (2, 1, 3), (3, 0, 1), (1, 1, 4), (3, 0, 2), (2, 1, 4)),
        ((1, 0, 3), (0, 1, 4), (2, 0, 3), (0, 1, 5), (4, 0, 0), (3, 1, 2)),
        (),
        (),
        ((1, 1, 5), (3, 0, 3)),
        (),
        (),
        (),
        (),
        ((4, 0, 1), (2, 1, 5)),
        (),
        (),
        (),
        ((4, 0, 2), (3, 1, 3)),
        (),
        (),
        ((3, 1, 4), (5, 0, 0)),
        (),
        (),
        (),
        (),
        ((5, 0, 1), (4, 1, 0)),
        (),
        (),
        ((5, 0, 2), (3, 1, 5), (6, 1, 1), (4, 1, 1), (6, 1, 2), (4, 1, 2), (6, 1, 3), (4, 1, 3), (6, 1, 4), (4, 1, 4), (5, 1, 0), (4, 0, 3), (5, 1, 1), (8, 1, 1), (5, 1, 2)),
        (),
        (),
        ((4, 1, 5), (8, 1, 2)),
        (),
        (),
        (),
        (),
        (),
        ((8, 1, 3), (8, 0, 2)),
        ((8, 1, 4), (8, 0, 3), (8, 0, 4), (5, 0, 3), (5, 1, 3), (10, 1, 1), (5, 1, 4), (10, 1, 2), (11, 1, 1), (10, 0, 2), (11, 1, 2), (11, 0, 2)),
        (),
        (),
        ((5, 1, 5), (10, 1, 3)),
        ((10, 0, 3), (11, 1, 3)),
        (),
        (),
        (),
        ((10, 1, 4),),
        (),
        ((6, 0, 2), (11, 1, 4)),
        ((11, 0, 3), (10, 0, 4), (6, 0, 3)),
        (),
        ((11, 0, 4), (12, 1, 1), (12, 1, 2), (6, 0, 4), (13, 1, 1), (12, 0, 2), (13, 1, 2), (12, 1, 3), (13, 0, 2), (12, 0, 3)),
        ((13, 0, 3), (13, 1, 3)),
        ((12, 0, 4), (12, 1, 4), (13, 1, 4), (13, 0, 4)),
        (),
    ),
    (
        (),
        ((14, 0, 0),),
        ((0, 1, 0),),
        ((0, 1, 1), (0, 0, 2), (2, 1, 0)),
        (),
        ((1, 1, 0), (15, 0, 0)),
        (),
        ((0, 0, 3), (0, 1, 2), (2, 1, 1), (1, 1, 1)),
        ((3, 1, 0), (1, 0, 2), (1, 1, 2), (2, 0, 2), (2, 1, 2), (1, 0, 3), (0, 1, 3), (2, 0, 3), (3, 1, 1), (1, 0, 4), (3, 1, 2), (2, 0, 4)),
        ((1, 1, 3), (0, 0, 4), (2, 1, 3), (0, 0, 5), (4, 1, 0), (3, 0, 2)),
        (),
        (),
        ((1, 0, 5), (3, 1, 3)),
        (),
        (),
        (),
        (),
        ((4, 1, 1),),
        ((2, 0, 5),),
        (),
        (),
        ((4, 1, 2), (3, 0, 3)),
        (),
        (),
        ((3, 0, 4), (5, 1, 0)),
        (),
        (),
        (),
        (),
        ((5, 1, 1),),
        ((4, 0, 0),),
        (),
        ((5, 1, 2), (3, 0, 5), (6, 0, 1), (4, 0, 1), (6, 0, 2), (4, 0, 2), (6, 0, 3), (4, 0, 3), (6, 0, 4), (4, 0, 4), (5, 0, 0), (4, 1, 3), (5, 0, 1), (8, 0, 1), (5, 0, 2)),
        (),
        (),
        ((4, 0, 5), (8, 0, 2)),
        (),
        (),
        (),
        (),
        (),
        ((8, 0, 3), (8, 1, 2)),
        ((8, 0, 4), (8, 1, 3), (8, 1, 4), (5, 1, 3), (5, 0, 3), (10, 0, 1), (5, 0, 4), (10, 0, 2), (11, 0, 1), (10, 1, 2), (11, 0, 2), (11, 1, 2)),
        (),
        (),
        ((5, 0, 5), (10, 0, 3)),
        ((10, 1, 3), (11, 0, 3)),
        (),
        (),
        (),
        ((10, 0, 4),),
        (),
        ((6, 1, 2), (11, 0, 4)),
        ((11, 1, 3), (10, 1, 4), (6, 1, 3)),
        (),
        ((11, 1, 4), (12, 0, 1), (12, 0, 2), (6, 1, 4), (13, 0, 1), (12, 1, 2), (13, 0, 2), (12, 0, 3), (13, 1, 2), (12, 1, 3)),
        ((13, 0, 3), (13, 1, 3)),
        ((12, 0, 4), (12, 1, 4), (13, 0, 4), (13, 1, 4)),
        (),
    ),
    (
        (),
        (),
        ((0, 0, 0), (0, 1, 0)),
        ((0, 1, 1), (2, 1, 0)),
        (),
        ((1, 0, 0), (1, 1, 0)),
        ((2, 0, 0), (0, 0, 1), (3, 1, 0), (1, 1, 1), (3, 0, 0), (2, 1, 1), (0, 1, 2)),
        ((1, 0, 1), (2, 0, 1)),
        ((3, 1, 1), (5, 1, 0), (5, 0, 0), (1, 1, 2), (3, 0, 1), (2, 1, 2), (4, 1, 0), (4, 0, 0), (3, 1, 2), (4, 1, 1), (5, 1, 1)),
        (),
        (),
        (),
        (),
        (),
        (),
        (),
        (),
        (),
        (),
        (),
        ((6, 0, 0), (6, 0, 1)),
        ((6, 0, 2), (4, 0, 1), (6, 0, 3)),
        ((6, 0, 4),),
        (),
        (),
        (),
        ((4, 1, 2),),
        (),
        (),
        (),
        (),
        (),
        ((8, 0, 0), (8, 0, 1), (8, 0, 2), (5, 0, 1), (8, 0, 3), (8, 0, 4), (5, 1, 2)),
        (),
        (),
        (),
        (),
        (),
        ((8, 1, 3),),
        ((10, 0, 0), (10, 0, 1)),
        (),
        (),
        ((8, 1, 4), (11, 0, 0), (11, 0, 1), (8, 0, 5), (10, 0, 2)),
        ((11, 0, 2), (10, 0, 3), (11, 0, 3), (10, 1, 3), (11, 1, 3), (10, 0, 4), (11, 0, 4)),
        ((10, 0, 5),),
        ((11, 0, 5), (10, 1, 4)),
        (),
        (),
        (),
        (),
        ((12, 0, 0),),
        ((12, 0, 1),),
        ((6, 1, 3),),
        ((11, 1, 4), (13, 0, 0), (13, 0, 1), (12, 0, 2), (6, 0, 5), (6, 1, 4)),
        ((13, 0, 2),),
        ((12, 0, 3),),
        ((12, 1, 3), (13, 0, 3), (13, 1, 3), (12, 0, 4), (13, 0, 4), (12, 1, 4)),
        ((13, 1, 4), (12, 0, 5), (13, 0, 5)),
        (),
    ),
)


def mirrored(index):
    return 7 - index if index < 8 else index


def out_plan(right, k):
    plan = []
    for q in range(4):
        place = q if right else 3 - q
        active, src, dst = False, 0, 0
        if place < 2 and k < place + 3:
            active, src = True, place - k + 2
            dst = src
        elif place == 2:
            active = True
            src, dst = (OTHER, PASS) if k == 0 else (5 - k, 5 - k)
        elif place == 3 and k < 2:
            active, src, dst = True, OTHER + k, 1 - k
        if not right:
            src, dst = mirrored(src), mirrored(dst)
        plan.append((active, src, dst))
    return plan


def back_plan(left, k):
    plan = []
    for q in range(4):
        place = q if left else 3 - q
        active, src, dst, added = False, 0, 0, -1
        if 3 - place <= k <= 4:
            index = k - 3 + place
            active = True
            src = index if left else 7 - index
            slot = RECV + index if left else 16 - index
            dst = slot if place > 0 else TRANSIT - index
            added = slot if place < 3 else -1
        elif place == 3 and k == 5:
            active, src, dst = True, TRANSIT, HOME
        plan.append((active, src, dst, added))
    return plan


def kernel(
    held_fwd,
    held_grad,
    saved,
    ids_f_hbm,
    probs_f_hbm,
    ids_b_hbm,
    probs_b_hbm,
    w_gate_hbm,
    w_up_hbm,
    w_down_hbm,
    out_f,
    out_b,
    saved_rows,
    ids_f,
    probs_f,
    ids_b,
    probs_b,
    result,
    w_gate,
    w_up,
    w_down,
    x_rows,
    g_rows,
    y_out,
    y_back,
    raw,
    edge_out,
    blk,
    ret,
    lhs,
    act,
    pre,
    total,
    gathering,
    scattering,
    w_sem,
    in_sem,
    out_sem,
    shift_send,
    shift_recv,
    y_send_sem,
    y_recv_sem,
    raw_send_sem,
    raw_recv_sem,
    edge_send_sem,
    edge_recv_sem,
    out_send_sem,
    out_recv_sem,
    back_send_sem,
    back_recv_sem,
):
    pipe = lax.axis_index("pipe")
    position = lax.axis_index("expert")
    plane = position // 8
    z = position % 8
    half = z // 4
    q = z % 4
    right = (pipe, plane * 8 + (z + 1) % 8)
    left = (pipe, plane * 8 + (z + 7) % 8)
    across = (pipe, (1 - plane) * 8 + z)
    after = ((pipe + 1) % 16, position)
    before = ((pipe + 15) % 16, position)

    barrier = pltpu.get_barrier_semaphore()
    for device in (right, left, across, after, before):
        pl.semaphore_signal(barrier, inc=1, device_id=device, device_id_type=MESH)

    input_copies = [
        pltpu.make_async_copy(src, dst, in_sem.at[n])
        for n, (src, dst) in enumerate(
            (
                (ids_b_hbm, ids_b),
                (probs_b_hbm, probs_b),
                (saved, saved_rows),
                (ids_f_hbm, ids_f),
                (probs_f_hbm, probs_f),
            )
        )
    ]
    for copy in input_copies:
        copy.start()
    weight_copies = [
        pltpu.make_async_copy(w_gate_hbm, w_gate, w_sem.at[0]),
        pltpu.make_async_copy(w_up_hbm, w_up, w_sem.at[1]),
        pltpu.make_async_copy(w_down_hbm, w_down, w_sem.at[2]),
    ]
    for copy in weight_copies:
        copy.start()

    def remote(src, dst, send_sem, recv_sem, device):
        return pltpu.make_async_remote_copy(
            src_ref=src,
            dst_ref=dst,
            send_sem=send_sem,
            recv_sem=recv_sem,
            device_id=device,
            device_id_type=MESH,
        )

    def grid(rows, cols):
        return (
            lax.broadcasted_iota(jnp.int32, (rows, cols), 0),
            lax.broadcasted_iota(jnp.int32, (rows, cols), 1),
        )

    def hot(mask):
        return jnp.where(mask, jnp.float32(1), jnp.float32(0)).astype(BF16)

    def dot(a, b):
        return jnp.dot(a, b, preferred_element_type=F32)

    def dot_t(a, b):
        return lax.dot_general(a, b, (((1,), (1,)), ((), ())), preferred_element_type=F32)

    def part_of(ref, position):
        base = pl.multiple_of((position // 2) * 128, 128)
        both = ref[:, pl.ds(base, 128)].astype(F32)
        return jnp.where(position % 2 == 0, both[:, :TOK], both[:, TOK:])

    def upright(row):
        i, j = grid(TOK, TOK)
        return jnp.sum(jnp.where(i == j, row, jnp.float32(0)), axis=1, keepdims=True)

    def routing(ids_ref, probs_ref, position):
        row = part_of(ids_ref, position)
        col = upright(row)
        i, j = grid(TOK, TOK)
        one, none = jnp.float32(1), jnp.float32(0)
        rank_row = jnp.sum(jnp.where((row == col) & (i < j), one, none), axis=0, keepdims=True)
        rank_col = jnp.sum(jnp.where((row == col) & (j < i), one, none), axis=1, keepdims=True)
        return row * SLOT + rank_row, col * SLOT + rank_col, upright(part_of(probs_ref, position))

    sources = (saved_rows, g_rows, x_rows)

    def choose(rows, slot_row, blocks):
        experts = [2 * side + line for side in (plane, 1 - plane) for line in (half, 1 - half)]
        i, j = grid(ROWS, 2 * TOK)
        slots = jnp.concatenate([slot_row, slot_row], axis=1)
        slots = jnp.where((i < SLOT) == (j < TOK), slots, jnp.float32(-1))
        offset = jnp.where(i < SLOT, i, i - SLOT)
        maps = [
            jnp.where((offset + expert * SLOT).astype(F32) == slots, jnp.float32(1), jnp.float32(0))
            for expert in experts
        ]
        maps = jnp.concatenate(maps, axis=0).astype(BF16)
        for c in STARTS:
            upper = rows[:, c : c + WIDE]
            lower = rows[:, HALF + c : HALF + c + WIDE]
            value = dot(maps, jnp.concatenate([upper, lower], axis=0))
            for n in range(4):
                blocks[n][:, c : c + WIDE] = value[n * ROWS : (n + 1) * ROWS].astype(BF16)

    on_edge = (q == 0) | (q == 3)
    near = jnp.where(q == 3, 4, 3)

    def choose_own(t, slot_row):
        side = (S_A, G_A, X_A)[t]
        blocks = (blk.at[side, q + 2], blk.at[side, OTHER], y_out.at[t, 0], y_out.at[t, 1])
        choose(sources[t], slot_row, blocks)

    def choose_near(t, slot_row):
        side = (S_A, G_A, X_A)[t]
        blocks = (blk.at[side, near], blk.at[side, PASS], edge_out.at[t, 0], edge_out.at[t, 1])
        choose(raw.at[t], slot_row, blocks)

    def edge_copy(t, n):
        side = (S_B, G_B, X_B)[t]
        place = near if n == 0 else PASS
        return remote(
            edge_out.at[t, n],
            blk.at[side, place],
            edge_send_sem.at[t, n],
            edge_recv_sem.at[t, n],
            across,
        )

    def raw_copy(t, way):
        rows = saved if t == 0 else sources[t]
        return remote(
            rows, raw.at[t], raw_send_sem.at[t], raw_recv_sem.at[t], right if way == 0 else left
        )

    def y_copy(t, n):
        side = (S_B, G_B, X_B)[t]
        place = q + 2 if n == 0 else OTHER
        return remote(
            y_out.at[t, n], blk.at[side, place], y_send_sem.at[t, n], y_recv_sem.at[t, n], across
        )

    def columns(t, p):
        if PARTS[t] == 1:
            return pl.ds(0, HALF)
        return pl.ds(0, 4 * WIDE) if p == 0 else pl.ds(4 * WIDE, 3 * WIDE)

    def out_copy(t, way, k, src, dst):
        return remote(
            blk.at[t, src],
            blk.at[t, dst],
            out_send_sem.at[t, way, k],
            out_recv_sem.at[t, dst],
            right if way == 0 else left,
        )

    def back_copy(t, p, way, k, src, dst):
        return remote(
            ret.at[t, src, :, columns(t, p)],
            ret.at[t, dst, :, columns(t, p)],
            back_send_sem.at[t, p, way, k],
            back_recv_sem.at[t, p, dst],
            left if way == 0 else right,
        )

    arrived = [set() for _ in range(4)]
    started = [([], []) for _ in range(4)]

    def need(place, key):
        if key in arrived[place]:
            return
        arrived[place].add(key)
        picked = key[0] == "out" and place in (0, 3) and TENSOR[key[1]] in RAWS
        if key[0] == "raw":
            raw_copy(key[1], 0).wait_recv()
        elif picked and key[2] in (4 if place == 3 else 3, PASS):
            if key[1] in (S_B, G_B, X_B):
                edge_copy(TENSOR[key[1]], 0 if key[2] < 8 else 1).wait_recv()
        elif key[0] == "out":
            out_copy(key[1], 0, 0, key[2], key[2]).wait_recv()
        elif key[0] == "back":
            back_copy(key[1], key[2], 0, 0, key[3], key[3]).wait_recv()
        elif key[1] in (S_B, G_B, X_B):
            y_copy(TENSOR[key[1]], key[2]).wait_recv()

    def described(place, op):
        stream, way, k = op
        if stream >= 14:
            return raw_copy(stream - 14, way)
        if stream < 6:
            _, src, dst = out_plan(way == 0, k)[place]
            return out_copy(stream, way, k, src, dst)
        t, p = (stream - 6) // 2, (stream - 6) % 2
        _, src, dst, _ = back_plan(way == 0, k)[place]
        return back_copy(t, p, way, k, src, dst)

    def start(place, op):
        stream, way, k = op
        if stream < 6:
            _, src, _ = out_plan(way == 0, k)[place]
            if src == place + 2:
                need(place, ("own", stream, 0))
            elif src == OTHER:
                need(place, ("own", stream, 1))
            else:
                need(place, ("out", stream, src))
        elif stream < 14:
            t, p = (stream - 6) // 2, (stream - 6) % 2
            _, src, _, added = back_plan(way == 0, k)[place]
            if src == TRANSIT:
                need(place, ("back", t, p, TRANSIT))
            if added >= 0:
                need(place, ("back", t, p, added))
                cols = columns(t, p)
                joined = ret[t, src, :, cols].astype(F32) + ret[t, added, :, cols].astype(F32)
                ret[t, src, :, cols] = joined.astype(BF16)
        link = started[place][(way == 0) == (stream < 6 or stream >= 14)]
        if len(link) >= DEPTH:
            described(place, link[-DEPTH]).wait_send()
        link.append(op)
        described(place, op).start()

    def all_of(*sides):
        def keys(place):
            found = []
            for side in sides:
                found.append(("own", side, 0))
                found += [("out", side, i) for i in range(8) if i != place + 2]
            return found

        return keys

    def home_of(t, parts):
        def keys(place):
            found = []
            for p in parts:
                found.append(("back", t, p, HOME))
                if place < 3:
                    found.append(("back", t, p, RECV + place + 2))
                if place > 0:
                    found.append(("back", t, p, RECV + place + 3))
            return found

        return keys

    def nothing(place):
        return []

    count = [0]

    def piece(keys=nothing):
        number = count[0]
        count[0] += 1
        for place in range(4):
            ops = ORDER[place][number]
            if ops or any(key not in arrived[place] for key in keys(place)):

                @pl.when(q == place)
                def _():
                    for op in ops:
                        start(place, op)
                    for key in keys(place):
                        need(place, key)

    def gather(t, to):
        for c in STARTS:
            rows = [blk[t, i, :, c : c + WIDE].astype(F32) for i in range(8)]
            value = dot(gathering[...], jnp.concatenate(rows, axis=0).astype(BF16)).astype(BF16)
            lhs[to, :, c : c + WIDE] = value[:ALL]
            lhs[to, :, HALF + c : HALF + c + WIDE] = value[ALL:]

    def scatter(t, c, upper, lower):
        both = jnp.concatenate([upper, lower], axis=0).astype(BF16)
        value = dot(scattering[...], both)
        for i in range(8):
            ret[t, i, :, c : c + WIDE] = value[i * ROWS : (i + 1) * ROWS].astype(BF16)

    def hidden_bwd():
        pre[0] = dot(lhs[0], w_gate[...])
        piece()
        pre[1] = dot(lhs[0], w_up[...])
        piece()
        dh = dot_t(lhs[1], w_down[...])
        gate, up = pre[0], pre[1]
        s = jax.nn.sigmoid(gate)
        act[0] = (dh * up * s * (1.0 + gate * (1.0 - s))).astype(BF16)
        act[1] = (dh * gate * s).astype(BF16)

    def rows_bwd(t):
        for c in STARTS:
            piece()
            values = []
            for n in (slice(c, c + WIDE), slice(HALF + c, HALF + c + WIDE)):
                values.append(dot_t(act[0], w_gate[n, :]) + dot_t(act[1], w_up[n, :]))
            scatter(t, c, *values)

    def hidden_fwd():
        pre[0] = dot(lhs[0], w_gate[...])
        piece()
        gate = pre[0]
        up = dot(lhs[0], w_up[...])
        act[0] = (gate * jax.nn.sigmoid(gate) * up).astype(BF16)

    def rows_fwd(t):
        for c in STARTS:
            piece()
            upper = dot(act[0], w_down[:, c : c + WIDE])
            lower = dot(act[0], w_down[:, HALF + c : HALF + c + WIDE])
            scatter(t, c, upper, lower)

    def join_home(t, cols):
        place = q + 2

        def joined(*others):
            value = ret[t, place, :, cols].astype(F32)
            for other in others:
                value = value + ret[t, other, :, cols].astype(F32)
            ret[t, place, :, cols] = value.astype(BF16)

        pl.when(q == 0)(lambda: joined(RECV + place))
        pl.when((q > 0) & (q < 3))(lambda: joined(RECV + place, RECV + place + 1))
        pl.when(q == 3)(lambda: joined(RECV + place + 1))

    def y_back_copy(t, n):
        src = ret.at[(R_B, F_B)[t], q + 2 if n == 0 else HOME]
        return remote(
            src, y_back.at[t, n], y_send_sem.at[3 + t, n], y_recv_sem.at[3 + t, n], across
        )

    def home_b(t):
        join_home((R_B, F_B)[t], pl.ds(0, HALF))
        for n in (0, 1):
            y_back_copy(t, n).start()

    def combine(t, slot_col, owner, blocks, base, out, starts):
        i, j = grid(2 * TOK, 2 * ROWS)
        within = jnp.where(j < ROWS, j, j - ROWS)
        first = (2 * owner + jnp.where(j < ROWS, half, 1 - half)) * SLOT
        slot = first + jnp.where(within < SLOT, within, within - SLOT)
        slots = jnp.concatenate([slot_col, slot_col], axis=0)
        maps = hot((slot.astype(F32) == slots) & ((within < SLOT) == (i < TOK)))
        scale = probs_col[t]
        for c in starts:
            both = [block[:, c : c + WIDE].astype(F32) for block in blocks]
            value = dot(maps, jnp.concatenate(both, axis=0).astype(BF16))
            for n, at in ((slice(c, c + WIDE), 0), (slice(HALF + c, HALF + c + WIDE), TOK)):
                added = base[:, n].astype(F32) + scale * value[at : at + TOK]
                out[:, n] = added.astype(out.dtype)

    def combine_b(t):
        for n in (0, 1):
            y_back_copy(t, n).wait_recv()
        blocks = (y_back.at[t, 0], y_back.at[t, 1])
        combine(t, slot_cols[t], 1 - plane, blocks, (g_rows, x_rows)[t], total.at[t], STARTS)

    def output_copies(t, p=None):
        ends = (0, HALF) if p is None or PARTS[F_A] == 1 else ((0, 4 * WIDE), (4 * WIDE, HALF))[p]
        return [
            pltpu.make_async_copy(
                result.at[t, :, pl.ds(side + ends[0], ends[1] - ends[0])],
                (out_b, out_f)[t].at[:, pl.ds(side + ends[0], ends[1] - ends[0])],
                out_sem.at[t, p or 0, n],
            )
            for n, side in enumerate((0, HALF))
        ]

    def combine_a(t, p=None):
        side = (R_A, F_A)[t]
        join_home(side, pl.ds(0, HALF) if p is None else columns(side, p))
        starts = STARTS if p is None or PARTS[side] == 1 else (STARTS[:4], STARTS[4:])[p]
        blocks = (ret.at[side, q + 2], ret.at[side, HOME])
        combine(t, slot_cols[t], plane, blocks, total.at[t], result.at[t], starts)

    shift_g = remote(held_grad, g_rows, shift_send.at[0], shift_recv.at[0], before)
    shift_x = remote(held_fwd, x_rows, shift_send.at[1], shift_recv.at[1], after)

    def crossing(t, act):
        act(y_copy(t, 0))
        if t in RAWS:
            pl.when(on_edge)(lambda: act(y_copy(t, 1)))
        else:
            act(y_copy(t, 1))

    def cross(t):
        crossing(t, lambda copy: copy.start())

    def raw_of(t):
        return lambda place: [("raw", t)] if place in (0, 3) else []

    def pick_near(t):
        if t not in RAWS:
            return
        piece(raw_of(t))

        @pl.when(on_edge)
        def _():
            choose_near(t, (near_b, near_b, near_f)[t])
            for n in (0, 1):
                edge_copy(t, n).start()

    piece()
    pl.semaphore_wait(barrier, 5)
    shift_g.start()

    piece()
    for copy in input_copies:
        copy.wait()
    slot_row_b, slot_col_b, prob_b = routing(ids_b, probs_b, position)
    choose_own(0, slot_row_b)

    piece()
    slot_row_f, slot_col_f, prob_f = routing(ids_f, probs_f, position)
    neighbour = position + jnp.where(q == 0, 1, 0) - jnp.where(q == 3, 1, 0)
    near_b = routing(ids_b, probs_b, neighbour)[0]
    near_f = routing(ids_f, probs_f, neighbour)[0]
    slot_cols = (slot_col_b, slot_col_f)
    probs_col = (prob_b, prob_f)
    for way, ref in ((0, gathering), (1, scattering)):
        i, j = grid(2 * ALL, 2 * ALL)
        packed, whole = (j, i) if way == 0 else (i, j)
        within = lax.rem(packed, ROWS)
        goal = lax.div(packed, ROWS) * SLOT + lax.rem(within, SLOT)
        goal = goal + jnp.where(within >= SLOT, ALL, 0)
        ref[...] = hot(goal == whole)
    cross(0)

    piece()
    shift_g.wait_recv()

    piece()
    choose_own(1, slot_row_b)
    cross(1)
    shift_x.start()
    pick_near(0)
    pick_near(1)

    piece()
    shift_x.wait_recv()
    choose_own(2, slot_row_f)
    cross(2)

    for saved_side, grad_side, back in ((S_A, G_A, R_A), (S_B, G_B, R_B)):
        piece(all_of(saved_side))
        gather(saved_side, 0)
        piece(all_of(grad_side))
        gather(grad_side, 1)
        if back == R_A:
            for copy in weight_copies:
                copy.wait()
        piece()
        hidden_bwd()
        rows_bwd(back)
        if back == R_A:
            pick_near(2)

    piece(all_of(X_B))
    gather(X_B, 0)
    piece()
    hidden_fwd()
    rows_fwd(F_B)

    piece(home_of(R_B, range(PARTS[R_B])))
    home_b(0)

    piece(all_of(X_A))
    gather(X_A, 0)
    piece()
    hidden_fwd()
    rows_fwd(F_A)

    piece(home_of(F_B, range(PARTS[F_B])))
    home_b(1)
    piece()
    combine_b(0)
    piece(home_of(R_A, range(PARTS[R_A])))
    combine_a(0)
    for copy in output_copies(0):
        copy.start()
    piece()
    combine_b(1)
    for p in range(PARTS[F_A]):
        piece(home_of(F_A, (p,)))
        combine_a(1, p)
        for copy in output_copies(1, p):
            copy.start()

    shift_g.wait_send()
    shift_x.wait_send()
    for t in range(3):
        crossing(t, lambda copy: copy.wait_send())
    for t in range(2):
        for n in (0, 1):
            y_back_copy(t, n).wait_send()
    for t in RAWS:
        for n in (0, 1):
            pl.when(on_edge)(lambda: edge_copy(t, n).wait_send())
    for place in range(4):

        @pl.when(q == place)
        def _():
            for link in started[place]:
                for op in link[-DEPTH:]:
                    described(place, op).wait_send()

    for copy in output_copies(0):
        copy.wait()
    for p in range(PARTS[F_A]):
        for copy in output_copies(1, p):
            copy.wait()


def give(from_f, from_b, to_f, to_b):
    to_f[...] = from_f[...]
    to_b[...] = from_b[...]


def on_device(
    held_fwd, ids_fwd, probs_fwd, saved_in, held_grad, ids_bwd, probs_bwd, w_gate, w_up, w_down
):
    vmem = pl.BlockSpec(memory_space=pltpu.VMEM)
    hbm = pl.BlockSpec(memory_space=pl.ANY)
    rows = jax.ShapeDtypeStruct((TOK, D), BF16)
    fwd, grad = pl.pallas_call(
        kernel,
        out_shape=(rows, rows),
        in_specs=[hbm] * 10,
        out_specs=(hbm, hbm),
        scratch_shapes=[
            pltpu.VMEM((TOK, D), BF16),
            pltpu.VMEM((1, TOKENS), jnp.int32),
            pltpu.VMEM((1, TOKENS), BF16),
            pltpu.VMEM((1, TOKENS), jnp.int32),
            pltpu.VMEM((1, TOKENS), BF16),
            pltpu.VMEM((2, TOK, D), BF16),
            pltpu.VMEM((D, HID), BF16),
            pltpu.VMEM((D, HID), BF16),
            pltpu.VMEM((HID, D), BF16),
            pltpu.VMEM((TOK, D), BF16),
            pltpu.VMEM((TOK, D), BF16),
            pltpu.VMEM((3, 2, ROWS, HALF), BF16),
            pltpu.VMEM((2, 2, ROWS, HALF), BF16),
            pltpu.VMEM((3, TOK, D), BF16),
            pltpu.VMEM((3, 2, ROWS, HALF), BF16),
            pltpu.VMEM((6, 10, ROWS, HALF), BF16),
            pltpu.VMEM((4, 19, ROWS, HALF), BF16),
            pltpu.VMEM((2, ALL, D), BF16),
            pltpu.VMEM((2, ALL, HID), BF16),
            pltpu.VMEM((2, ALL, HID), F32),
            pltpu.VMEM((2, TOK, D), F32),
            pltpu.VMEM((2 * ALL, 2 * ALL), BF16),
            pltpu.VMEM((2 * ALL, 2 * ALL), BF16),
            pltpu.SemaphoreType.DMA((3,)),
            pltpu.SemaphoreType.DMA((5,)),
            pltpu.SemaphoreType.DMA((2, 2, 2)),
            pltpu.SemaphoreType.DMA((2,)),
            pltpu.SemaphoreType.DMA((2,)),
            pltpu.SemaphoreType.DMA((5, 2)),
            pltpu.SemaphoreType.DMA((5, 2)),
            pltpu.SemaphoreType.DMA((3,)),
            pltpu.SemaphoreType.DMA((3,)),
            pltpu.SemaphoreType.DMA((3, 2)),
            pltpu.SemaphoreType.DMA((3, 2)),
            pltpu.SemaphoreType.DMA((6, 2, STEPS)),
            pltpu.SemaphoreType.DMA((6, 10)),
            pltpu.SemaphoreType.DMA((4, 2, 2, STEPS)),
            pltpu.SemaphoreType.DMA((4, 2, 19)),
        ],
        compiler_params=pltpu.CompilerParams(
            collective_id=0, has_side_effects=True, vmem_limit_bytes=60 * 2**20
        ),
        cost_estimate=pl.CostEstimate(
            flops=7_050_000_000, bytes_accessed=12_000_000, transcendentals=300_000
        ),
        name="relay_experts",
    )(
        held_fwd[0],
        held_grad[0],
        saved_in[0],
        ids_fwd,
        probs_fwd,
        ids_bwd,
        probs_bwd,
        w_gate[0],
        w_up[0],
        w_down[0],
    )
    fwd, grad = pl.pallas_call(
        give,
        out_shape=(rows, rows),
        in_specs=[vmem, vmem],
        out_specs=(vmem, vmem),
        name="give",
    )(fwd, grad)
    return (fwd[None], grad[None])


def solution(mesh):
    return jax.shard_map(
        on_device,
        mesh=mesh,
        in_specs=(
            P("pipe", "expert", None),
            P("pipe", None),
            P("pipe", None),
            P("pipe", "expert", None),
            P("pipe", "expert", None),
            P("pipe", None),
            P("pipe", None),
            P("pipe", None, "expert"),
            P("pipe", None, "expert"),
            P("pipe", "expert", None),
        ),
        out_specs=(P("pipe", "expert", None), P("pipe", "expert", None)),
        check_vma=False,
    )
```

```python
import jax
import jax.numpy as jnp
from jax import lax
from jax.experimental import pallas as pl
from jax.experimental.pallas import tpu as pltpu
from jax.sharding import PartitionSpec as P

SLOT = 20
MESH = pl.DeviceIdType.MESH
F32 = jnp.float32
BF16 = jnp.bfloat16

D = 3584
HID = 384
TOK = 64
TOKENS = 1024
ROWS = 2 * SLOT
HALF = D // 2
WIDE = 256
STARTS = tuple(range(0, HALF, WIDE))
ALL = 8 * SLOT
STEPS = 6

OTHER, PASS = 8, 9
RECV, HOME, TRANSIT = 8, 17, 18
S_A, G_A, S_B, G_B, X_B, X_A = range(6)
R_A, R_B, F_B, F_A = range(4)
PARTS = (1, 1, 2, 2)
DEPTH = 3
RAWS = (0, 1)
TENSOR = (0, 1, 0, 1, 2, 2)

ORDER = (
    (
        (),
        (),
        ((0, 0, 0), (0, 1, 0)),
        ((0, 0, 1), (2, 0, 0)),
        (),
        ((1, 0, 0), (1, 1, 0)),
        ((2, 1, 0), (0, 1, 1), (3, 0, 0), (1, 0, 1), (3, 1, 0), (2, 0, 1), (0, 0, 2)),
        ((1, 1, 1), (2, 1, 1), (3, 0, 1)),
        ((5, 0, 0), (5, 1, 0), (1, 0, 2), (3, 1, 1), (2, 0, 2), (4, 0, 0), (4, 1, 0), (3, 0, 2), (4, 0, 1), (5, 0, 1)),
        (),
        (),
        (),
        (),
        (),
        (),
        (),
        (),
        (),
        (),
        (),
        ((6, 1, 0), (6, 1, 1)),
        ((6, 1, 2), (4, 1, 1), (6, 1, 3)),
        ((6, 1, 4),),
        (),
        (),
        (),
        ((4, 0, 2),),
        (),
        (),
        (),
        (),
        (),
        ((8, 1, 0), (8, 1, 1), (8, 1, 2), (5, 1, 1), (8, 1, 3), (8, 1, 4), (5, 0, 2)),
        (),
        (),
        (),
        (),
        (),
        ((8, 0, 3),),
        ((10, 1, 0), (10, 1, 1)),
        (),
        (),
        ((8, 0, 4), (11, 1, 0), (11, 1, 1), (8, 1, 5), (10, 1, 2)),
        ((11, 1, 2), (10, 1, 3), (11, 1, 3), (10, 0, 3), (11, 0, 3), (10, 1, 4), (11, 1, 4)),
        ((10, 1, 5),),
        ((11, 1, 5), (10, 0, 4)),
        (),
        (),
        (),
        (),
        ((12, 1, 0),),
        ((12, 1, 1),),
        ((6, 0, 3),),
        ((11, 0, 4), (13, 1, 0), (13, 1, 1), (12, 1, 2), (6, 1, 5), (6, 0, 4)),
        ((13, 1, 2),),
        ((12, 1, 3),),
        ((12, 0, 3), (13, 1, 3), (13, 0, 3), (12, 1, 4), (13, 1, 4), (12, 0, 4)),
        ((13, 0, 4), (12, 1, 5), (13, 1, 5)),
        (),
    ),
    (
        (),
        ((14, 1, 0),),
        ((0, 0, 0),),
        ((0, 0, 1), (0, 1, 2), (2, 0, 0)),
        (),
        ((1, 0, 0), (15, 1, 0)),
        (),
        ((0, 1, 3), (0, 0, 2), (2, 0, 1), (1, 0, 1)),
        ((3, 0, 0), (1, 1, 2), (1, 0, 2), (2, 1, 2), (2, 0, 2), (1, 1, 3), (0, 0, 3), (2, 1, 3), (3, 0, 1), (1, 1, 4), (3, 0, 2), (2, 1, 4)),
        ((1, 0, 3), (0, 1, 4), (2, 0, 3), (0, 1, 5), (4, 0, 0), (3, 1, 2)),
        (),
        (),
        ((1, 1, 5), (3, 0, 3)),
        (),
        (),
        (),
        (),
        ((4, 0, 1), (2, 1, 5)),
        (),
        (),
        (),
        ((4, 0, 2), (3, 1, 3)),
        (),
        (),
        ((3, 1, 4), (5, 0, 0)),
        (),
        (),
        (),
        (),
        ((5, 0, 1), (4, 1, 0)),
        (),
        (),
        ((5, 0, 2), (3, 1, 5), (6, 1, 1), (4, 1, 1), (6, 1, 2), (4, 1, 2), (6, 1, 3), (4, 1, 3), (6, 1, 4), (4, 1, 4), (5, 1, 0), (4, 0, 3), (5, 1, 1), (8, 1, 1), (5, 1, 2)),
        (),
        (),
        ((4, 1, 5), (8, 1, 2)),
        (),
        (),
        (),
        (),
        (),
        ((8, 1, 3), (8, 0, 2)),
        ((8, 1, 4), (8, 0, 3), (8, 0, 4), (5, 0, 3), (5, 1, 3), (10, 1, 1), (5, 1, 4), (10, 1, 2), (11, 1, 1), (10, 0, 2), (11, 1, 2), (11, 0, 2)),
        (),
        (),
        ((5, 1, 5), (10, 1, 3)),
        ((10, 0, 3), (11, 1, 3)),
        (),
        (),
        (),
        ((10, 1, 4),),
        (),
        ((6, 0, 2), (11, 1, 4)),
        ((11, 0, 3), (10, 0, 4), (6, 0, 3)),
        (),
        ((11, 0, 4), (12, 1, 1), (12, 1, 2), (6, 0, 4), (13, 1, 1), (12, 0, 2), (13, 1, 2), (12, 1, 3), (13, 0, 2), (12, 0, 3)),
        ((13, 0, 3), (13, 1, 3)),
        ((12, 0, 4), (12, 1, 4), (13, 1, 4), (13, 0, 4)),
        (),
    ),
    (
        (),
        ((14, 0, 0),),
        ((0, 1, 0),),
        ((0, 1, 1), (0, 0, 2), (2, 1, 0)),
        (),
        ((1, 1, 0), (15, 0, 0)),
        (),
        ((0, 0, 3), (0, 1, 2), (2, 1, 1), (1, 1, 1)),
        ((3, 1, 0), (1, 0, 2), (1, 1, 2), (2, 0, 2), (2, 1, 2), (1, 0, 3), (0, 1, 3), (2, 0, 3), (3, 1, 1), (1, 0, 4), (3, 1, 2), (2, 0, 4)),
        ((1, 1, 3), (0, 0, 4), (2, 1, 3), (0, 0, 5), (4, 1, 0), (3, 0, 2)),
        (),
        (),
        ((1, 0, 5), (3, 1, 3)),
        (),
        (),
        (),
        (),
        ((4, 1, 1),),
        ((2, 0, 5),),
        (),
        (),
        ((4, 1, 2), (3, 0, 3)),
        (),
        (),
        ((3, 0, 4), (5, 1, 0)),
        (),
        (),
        (),
        (),
        ((5, 1, 1),),
        ((4, 0, 0),),
        (),
        ((5, 1, 2), (3, 0, 5), (6, 0, 1), (4, 0, 1), (6, 0, 2), (4, 0, 2), (6, 0, 3), (4, 0, 3), (6, 0, 4), (4, 0, 4), (5, 0, 0), (4, 1, 3), (5, 0, 1), (8, 0, 1), (5, 0, 2)),
        (),
        (),
        ((4, 0, 5), (8, 0, 2)),
        (),
        (),
        (),
        (),
        (),
        ((8, 0, 3), (8, 1, 2)),
        ((8, 0, 4), (8, 1, 3), (8, 1, 4), (5, 1, 3), (5, 0, 3), (10, 0, 1), (5, 0, 4), (10, 0, 2), (11, 0, 1), (10, 1, 2), (11, 0, 2), (11, 1, 2)),
        (),
        (),
        ((5, 0, 5), (10, 0, 3)),
        ((10, 1, 3), (11, 0, 3)),
        (),
        (),
        (),
        ((10, 0, 4),),
        (),
        ((6, 1, 2), (11, 0, 4)),
        ((11, 1, 3), (10, 1, 4), (6, 1, 3)),
        (),
        ((11, 1, 4), (12, 0, 1), (12, 0, 2), (6, 1, 4), (13, 0, 1), (12, 1, 2), (13, 0, 2), (12, 0, 3), (13, 1, 2), (12, 1, 3)),
        ((13, 0, 3), (13, 1, 3)),
        ((12, 0, 4), (12, 1, 4), (13, 0, 4), (13, 1, 4)),
        (),
    ),
    (
        (),
        (),
        ((0, 0, 0), (0, 1, 0)),
        ((0, 1, 1), (2, 1, 0)),
        (),
        ((1, 0, 0), (1, 1, 0)),
        ((2, 0, 0), (0, 0, 1), (3, 1, 0), (1, 1, 1), (3, 0, 0), (2, 1, 1), (0, 1, 2)),
        ((1, 0, 1), (2, 0, 1)),
        ((3, 1, 1), (5, 1, 0), (5, 0, 0), (1, 1, 2), (3, 0, 1), (2, 1, 2), (4, 1, 0), (4, 0, 0), (3, 1, 2), (4, 1, 1), (5, 1, 1)),
        (),
        (),
        (),
        (),
        (),
        (),
        (),
        (),
        (),
        (),
        (),
        ((6, 0, 0), (6, 0, 1)),
        ((6, 0, 2), (4, 0, 1), (6, 0, 3)),
        ((6, 0, 4),),
        (),
        (),
        (),
        ((4, 1, 2),),
        (),
        (),
        (),
        (),
        (),
        ((8, 0, 0), (8, 0, 1), (8, 0, 2), (5, 0, 1), (8, 0, 3), (8, 0, 4), (5, 1, 2)),
        (),
        (),
        (),
        (),
        (),
        ((8, 1, 3),),
        ((10, 0, 0), (10, 0, 1)),
        (),
        (),
        ((8, 1, 4), (11, 0, 0), (11, 0, 1), (8, 0, 5), (10, 0, 2)),
        ((11, 0, 2), (10, 0, 3), (11, 0, 3), (10, 1, 3), (11, 1, 3), (10, 0, 4), (11, 0, 4)),
        ((10, 0, 5),),
        ((11, 0, 5), (10, 1, 4)),
        (),
        (),
        (),
        (),
        ((12, 0, 0),),
        ((12, 0, 1),),
        ((6, 1, 3),),
        ((11, 1, 4), (13, 0, 0), (13, 0, 1), (12, 0, 2), (6, 0, 5), (6, 1, 4)),
        ((13, 0, 2),),
        ((12, 0, 3),),
        ((12, 1, 3), (13, 0, 3), (13, 1, 3), (12, 0, 4), (13, 0, 4), (12, 1, 4)),
        ((13, 1, 4), (12, 0, 5), (13, 0, 5)),
        (),
    ),
)


def mirrored(index):
    return 7 - index if index < 8 else index


def out_plan(right, k):
    plan = []
    for q in range(4):
        place = q if right else 3 - q
        active, src, dst = False, 0, 0
        if place < 2 and k < place + 3:
            active, src = True, place - k + 2
            dst = src
        elif place == 2:
            active = True
            src, dst = (OTHER, PASS) if k == 0 else (5 - k, 5 - k)
        elif place == 3 and k < 2:
            active, src, dst = True, OTHER + k, 1 - k
        if not right:
            src, dst = mirrored(src), mirrored(dst)
        plan.append((active, src, dst))
    return plan


def back_plan(left, k):
    plan = []
    for q in range(4):
        place = q if left else 3 - q
        active, src, dst, added = False, 0, 0, -1
        if 3 - place <= k <= 4:
            index = k - 3 + place
            active = True
            src = index if left else 7 - index
            slot = RECV + index if left else 16 - index
            dst = slot if place > 0 else TRANSIT - index
            added = slot if place < 3 else -1
        elif place == 3 and k == 5:
            active, src, dst = True, TRANSIT, HOME
        plan.append((active, src, dst, added))
    return plan


def kernel(
    held_fwd,
    held_grad,
    saved,
    ids_f_hbm,
    probs_f_hbm,
    ids_b_hbm,
    probs_b_hbm,
    w_gate_hbm,
    w_up_hbm,
    w_down_hbm,
    out_f,
    out_b,
    saved_rows,
    ids_f,
    probs_f,
    ids_b,
    probs_b,
    result,
    w_gate,
    w_up,
    w_down,
    x_rows,
    g_rows,
    y_out,
    y_back,
    raw,
    edge_out,
    blk,
    ret,
    lhs,
    act,
    pre,
    total,
    gathering,
    scattering,
    w_sem,
    in_sem,
    out_sem,
    shift_send,
    shift_recv,
    y_send_sem,
    y_recv_sem,
    raw_send_sem,
    raw_recv_sem,
    edge_send_sem,
    edge_recv_sem,
    out_send_sem,
    out_recv_sem,
    back_send_sem,
    back_recv_sem,
):
    pipe = lax.axis_index("pipe")
    position = lax.axis_index("expert")
    plane = position // 8
    z = position % 8
    half = z // 4
    q = z % 4
    right = (pipe, plane * 8 + (z + 1) % 8)
    left = (pipe, plane * 8 + (z + 7) % 8)
    across = (pipe, (1 - plane) * 8 + z)
    after = ((pipe + 1) % 16, position)
    before = ((pipe + 15) % 16, position)

    barrier = pltpu.get_barrier_semaphore()
    for device in (right, left, across, after, before):
        pl.semaphore_signal(barrier, inc=1, device_id=device, device_id_type=MESH)

    input_copies = [
        pltpu.make_async_copy(src, dst, in_sem.at[n])
        for n, (src, dst) in enumerate(
            (
                (ids_b_hbm, ids_b),
                (probs_b_hbm, probs_b),
                (saved, saved_rows),
                (ids_f_hbm, ids_f),
                (probs_f_hbm, probs_f),
            )
        )
    ]
    for copy in input_copies:
        copy.start()
    weight_copies = [
        pltpu.make_async_copy(w_gate_hbm, w_gate, w_sem.at[0]),
        pltpu.make_async_copy(w_up_hbm, w_up, w_sem.at[1]),
        pltpu.make_async_copy(w_down_hbm, w_down, w_sem.at[2]),
    ]

    def remote(src, dst, send_sem, recv_sem, device):
        return pltpu.make_async_remote_copy(
            src_ref=src,
            dst_ref=dst,
            send_sem=send_sem,
            recv_sem=recv_sem,
            device_id=device,
            device_id_type=MESH,
        )

    def grid(rows, cols):
        return (
            lax.broadcasted_iota(jnp.int32, (rows, cols), 0),
            lax.broadcasted_iota(jnp.int32, (rows, cols), 1),
        )

    def hot(mask):
        return jnp.where(mask, jnp.float32(1), jnp.float32(0)).astype(BF16)

    def dot(a, b):
        return jnp.dot(a, b, preferred_element_type=F32)

    def dot_t(a, b):
        return lax.dot_general(a, b, (((1,), (1,)), ((), ())), preferred_element_type=F32)

    def part_of(ref, position):
        base = pl.multiple_of((position // 2) * 128, 128)
        both = ref[:, pl.ds(base, 128)].astype(F32)
        return jnp.where(position % 2 == 0, both[:, :TOK], both[:, TOK:])

    def upright(row):
        i, j = grid(TOK, TOK)
        return jnp.sum(jnp.where(i == j, row, jnp.float32(0)), axis=1, keepdims=True)

    def routing(ids_ref, probs_ref, position):
        row = part_of(ids_ref, position)
        col = upright(row)
        i, j = grid(TOK, TOK)
        one, none = jnp.float32(1), jnp.float32(0)
        rank_row = jnp.sum(jnp.where((row == col) & (i < j), one, none), axis=0, keepdims=True)
        rank_col = jnp.sum(jnp.where((row == col) & (j < i), one, none), axis=1, keepdims=True)
        return row * SLOT + rank_row, col * SLOT + rank_col, upright(part_of(probs_ref, position))

    sources = (saved_rows, g_rows, x_rows)

    def choose(rows, slot_row, blocks):
        experts = [2 * side + line for side in (plane, 1 - plane) for line in (half, 1 - half)]
        i, j = grid(ROWS, 2 * TOK)
        slots = jnp.concatenate([slot_row, slot_row], axis=1)
        slots = jnp.where((i < SLOT) == (j < TOK), slots, jnp.float32(-1))
        offset = jnp.where(i < SLOT, i, i - SLOT)
        maps = [
            jnp.where((offset + expert * SLOT).astype(F32) == slots, jnp.float32(1), jnp.float32(0))
            for expert in experts
        ]
        maps = jnp.concatenate(maps, axis=0).astype(BF16)
        for c in STARTS:
            upper = rows[:, c : c + WIDE]
            lower = rows[:, HALF + c : HALF + c + WIDE]
            value = dot(maps, jnp.concatenate([upper, lower], axis=0))
            for n in range(4):
                blocks[n][:, c : c + WIDE] = value[n * ROWS : (n + 1) * ROWS].astype(BF16)

    on_edge = (q == 0) | (q == 3)
    near = jnp.where(q == 3, 4, 3)

    def choose_own(t, slot_row):
        side = (S_A, G_A, X_A)[t]
        blocks = (blk.at[side, q + 2], blk.at[side, OTHER], y_out.at[t, 0], y_out.at[t, 1])
        choose(sources[t], slot_row, blocks)

    def choose_near(t, slot_row):
        side = (S_A, G_A, X_A)[t]
        blocks = (blk.at[side, near], blk.at[side, PASS], edge_out.at[t, 0], edge_out.at[t, 1])
        choose(raw.at[t], slot_row, blocks)

    def edge_copy(t, n):
        side = (S_B, G_B, X_B)[t]
        place = near if n == 0 else PASS
        return remote(
            edge_out.at[t, n],
            blk.at[side, place],
            edge_send_sem.at[t, n],
            edge_recv_sem.at[t, n],
            across,
        )

    def raw_copy(t, way):
        rows = saved if t == 0 else sources[t]
        return remote(
            rows, raw.at[t], raw_send_sem.at[t], raw_recv_sem.at[t], right if way == 0 else left
        )

    def y_copy(t, n):
        side = (S_B, G_B, X_B)[t]
        place = q + 2 if n == 0 else OTHER
        return remote(
            y_out.at[t, n], blk.at[side, place], y_send_sem.at[t, n], y_recv_sem.at[t, n], across
        )

    def columns(t, p):
        if PARTS[t] == 1:
            return pl.ds(0, HALF)
        return pl.ds(0, 4 * WIDE) if p == 0 else pl.ds(4 * WIDE, 3 * WIDE)

    def out_copy(t, way, k, src, dst):
        return remote(
            blk.at[t, src],
            blk.at[t, dst],
            out_send_sem.at[t, way, k],
            out_recv_sem.at[t, dst],
            right if way == 0 else left,
        )

    def back_copy(t, p, way, k, src, dst):
        return remote(
            ret.at[t, src, :, columns(t, p)],
            ret.at[t, dst, :, columns(t, p)],
            back_send_sem.at[t, p, way, k],
            back_recv_sem.at[t, p, dst],
            left if way == 0 else right,
        )

    arrived = [set() for _ in range(4)]
    started = [([], []) for _ in range(4)]

    def need(place, key):
        if key in arrived[place]:
            return
        arrived[place].add(key)
        picked = key[0] == "out" and place in (0, 3) and TENSOR[key[1]] in RAWS
        if key[0] == "raw":
            raw_copy(key[1], 0).wait_recv()
        elif picked and key[2] in (4 if place == 3 else 3, PASS):
            if key[1] in (S_B, G_B, X_B):
                edge_copy(TENSOR[key[1]], 0 if key[2] < 8 else 1).wait_recv()
        elif key[0] == "out":
            out_copy(key[1], 0, 0, key[2], key[2]).wait_recv()
        elif key[0] == "back":
            back_copy(key[1], key[2], 0, 0, key[3], key[3]).wait_recv()
        elif key[1] in (S_B, G_B, X_B):
            y_copy(TENSOR[key[1]], key[2]).wait_recv()

    def described(place, op):
        stream, way, k = op
        if stream >= 14:
            return raw_copy(stream - 14, way)
        if stream < 6:
            _, src, dst = out_plan(way == 0, k)[place]
            return out_copy(stream, way, k, src, dst)
        t, p = (stream - 6) // 2, (stream - 6) % 2
        _, src, dst, _ = back_plan(way == 0, k)[place]
        return back_copy(t, p, way, k, src, dst)

    def start(place, op):
        stream, way, k = op
        if stream < 6:
            _, src, _ = out_plan(way == 0, k)[place]
            if src == place + 2:
                need(place, ("own", stream, 0))
            elif src == OTHER:
                need(place, ("own", stream, 1))
            else:
                need(place, ("out", stream, src))
        elif stream < 14:
            t, p = (stream - 6) // 2, (stream - 6) % 2
            _, src, _, added = back_plan(way == 0, k)[place]
            if src == TRANSIT:
                need(place, ("back", t, p, TRANSIT))
            if added >= 0:
                need(place, ("back", t, p, added))
                cols = columns(t, p)
                joined = ret[t, src, :, cols].astype(F32) + ret[t, added, :, cols].astype(F32)
                ret[t, src, :, cols] = joined.astype(BF16)
        link = started[place][(way == 0) == (stream < 6 or stream >= 14)]
        if len(link) >= DEPTH:
            described(place, link[-DEPTH]).wait_send()
        link.append(op)
        described(place, op).start()

    def all_of(*sides):
        def keys(place):
            found = []
            for side in sides:
                found.append(("own", side, 0))
                found += [("out", side, i) for i in range(8) if i != place + 2]
            return found

        return keys

    def home_of(t, parts):
        def keys(place):
            found = []
            for p in parts:
                found.append(("back", t, p, HOME))
                if place < 3:
                    found.append(("back", t, p, RECV + place + 2))
                if place > 0:
                    found.append(("back", t, p, RECV + place + 3))
            return found

        return keys

    def nothing(place):
        return []

    count = [0]

    def piece(keys=nothing):
        number = count[0]
        count[0] += 1
        for place in range(4):
            ops = ORDER[place][number]
            if ops or any(key not in arrived[place] for key in keys(place)):

                @pl.when(q == place)
                def _():
                    for op in ops:
                        start(place, op)
                    for key in keys(place):
                        need(place, key)

    def gather(t, to):
        for c in STARTS:
            rows = [blk[t, i, :, c : c + WIDE].astype(F32) for i in range(8)]
            value = dot(gathering[...], jnp.concatenate(rows, axis=0).astype(BF16)).astype(BF16)
            lhs[to, :, c : c + WIDE] = value[:ALL]
            lhs[to, :, HALF + c : HALF + c + WIDE] = value[ALL:]

    def scatter(t, c, upper, lower):
        both = jnp.concatenate([upper, lower], axis=0).astype(BF16)
        value = dot(scattering[...], both)
        for i in range(8):
            ret[t, i, :, c : c + WIDE] = value[i * ROWS : (i + 1) * ROWS].astype(BF16)

    def hidden_bwd():
        pre[0] = dot(lhs[0], w_gate[...])
        piece()
        pre[1] = dot(lhs[0], w_up[...])
        piece()
        dh = dot_t(lhs[1], w_down[...])
        gate, up = pre[0], pre[1]
        s = jax.nn.sigmoid(gate)
        act[0] = (dh * up * s * (1.0 + gate * (1.0 - s))).astype(BF16)
        act[1] = (dh * gate * s).astype(BF16)

    def rows_bwd(t):
        for c in STARTS:
            piece()
            values = []
            for n in (slice(c, c + WIDE), slice(HALF + c, HALF + c + WIDE)):
                values.append(dot_t(act[0], w_gate[n, :]) + dot_t(act[1], w_up[n, :]))
            scatter(t, c, *values)

    def hidden_fwd():
        pre[0] = dot(lhs[0], w_gate[...])
        piece()
        gate = pre[0]
        up = dot(lhs[0], w_up[...])
        act[0] = (gate * jax.nn.sigmoid(gate) * up).astype(BF16)

    def rows_fwd(t):
        for c in STARTS:
            piece()
            upper = dot(act[0], w_down[:, c : c + WIDE])
            lower = dot(act[0], w_down[:, HALF + c : HALF + c + WIDE])
            scatter(t, c, upper, lower)

    def join_home(t, cols):
        place = q + 2

        def joined(*others):
            value = ret[t, place, :, cols].astype(F32)
            for other in others:
                value = value + ret[t, other, :, cols].astype(F32)
            ret[t, place, :, cols] = value.astype(BF16)

        pl.when(q == 0)(lambda: joined(RECV + place))
        pl.when((q > 0) & (q < 3))(lambda: joined(RECV + place, RECV + place + 1))
        pl.when(q == 3)(lambda: joined(RECV + place + 1))

    def y_back_copy(t, n):
        src = ret.at[(R_B, F_B)[t], q + 2 if n == 0 else HOME]
        return remote(
            src, y_back.at[t, n], y_send_sem.at[3 + t, n], y_recv_sem.at[3 + t, n], across
        )

    def home_b(t):
        join_home((R_B, F_B)[t], pl.ds(0, HALF))
        for n in (0, 1):
            y_back_copy(t, n).start()

    def combine(t, slot_col, owner, blocks, base, out, starts):
        i, j = grid(2 * TOK, 2 * ROWS)
        within = jnp.where(j < ROWS, j, j - ROWS)
        first = (2 * owner + jnp.where(j < ROWS, half, 1 - half)) * SLOT
        slot = first + jnp.where(within < SLOT, within, within - SLOT)
        slots = jnp.concatenate([slot_col, slot_col], axis=0)
        maps = hot((slot.astype(F32) == slots) & ((within < SLOT) == (i < TOK)))
        scale = probs_col[t]
        for c in starts:
            both = [block[:, c : c + WIDE].astype(F32) for block in blocks]
            value = dot(maps, jnp.concatenate(both, axis=0).astype(BF16))
            for n, at in ((slice(c, c + WIDE), 0), (slice(HALF + c, HALF + c + WIDE), TOK)):
                added = base[:, n].astype(F32) + scale * value[at : at + TOK]
                out[:, n] = added.astype(out.dtype)

    def combine_b(t):
        for n in (0, 1):
            y_back_copy(t, n).wait_recv()
        blocks = (y_back.at[t, 0], y_back.at[t, 1])
        combine(t, slot_cols[t], 1 - plane, blocks, (g_rows, x_rows)[t], total.at[t], STARTS)

    def output_copies(t, p=None):
        ends = (0, HALF) if p is None or PARTS[F_A] == 1 else ((0, 4 * WIDE), (4 * WIDE, HALF))[p]
        return [
            pltpu.make_async_copy(
                result.at[t, :, pl.ds(side + ends[0], ends[1] - ends[0])],
                (out_b, out_f)[t].at[:, pl.ds(side + ends[0], ends[1] - ends[0])],
                out_sem.at[t, p or 0, n],
            )
            for n, side in enumerate((0, HALF))
        ]

    def combine_a(t, p=None):
        side = (R_A, F_A)[t]
        join_home(side, pl.ds(0, HALF) if p is None else columns(side, p))
        starts = STARTS if p is None or PARTS[side] == 1 else (STARTS[:4], STARTS[4:])[p]
        blocks = (ret.at[side, q + 2], ret.at[side, HOME])
        combine(t, slot_cols[t], plane, blocks, total.at[t], result.at[t], starts)

    shift_g = remote(held_grad, g_rows, shift_send.at[0], shift_recv.at[0], before)
    shift_x = remote(held_fwd, x_rows, shift_send.at[1], shift_recv.at[1], after)

    def crossing(t, act):
        act(y_copy(t, 0))
        if t in RAWS:
            pl.when(on_edge)(lambda: act(y_copy(t, 1)))
        else:
            act(y_copy(t, 1))

    def cross(t):
        crossing(t, lambda copy: copy.start())

    def raw_of(t):
        return lambda place: [("raw", t)] if place in (0, 3) else []

    def pick_near(t):
        if t not in RAWS:
            return
        piece(raw_of(t))

        @pl.when(on_edge)
        def _():
            choose_near(t, (near_b, near_b, near_f)[t])
            for n in (0, 1):
                edge_copy(t, n).start()

    piece()
    pl.semaphore_wait(barrier, 5)
    shift_g.start()

    piece()
    for copy in input_copies:
        copy.wait()
    for copy in weight_copies:
        copy.start()
    slot_row_b, slot_col_b, prob_b = routing(ids_b, probs_b, position)
    choose_own(0, slot_row_b)

    piece()
    slot_row_f, slot_col_f, prob_f = routing(ids_f, probs_f, position)
    neighbour = position + jnp.where(q == 0, 1, 0) - jnp.where(q == 3, 1, 0)
    near_b = routing(ids_b, probs_b, neighbour)[0]
    near_f = routing(ids_f, probs_f, neighbour)[0]
    slot_cols = (slot_col_b, slot_col_f)
    probs_col = (prob_b, prob_f)
    for way, ref in ((0, gathering), (1, scattering)):
        i, j = grid(2 * ALL, 2 * ALL)
        packed, whole = (j, i) if way == 0 else (i, j)
        within = lax.rem(packed, ROWS)
        goal = lax.div(packed, ROWS) * SLOT + lax.rem(within, SLOT)
        goal = goal + jnp.where(within >= SLOT, ALL, 0)
        ref[...] = hot(goal == whole)
    cross(0)

    piece()
    shift_g.wait_recv()

    piece()
    choose_own(1, slot_row_b)
    cross(1)
    shift_x.start()
    pick_near(0)
    pick_near(1)

    piece()
    shift_x.wait_recv()
    choose_own(2, slot_row_f)
    cross(2)

    for saved_side, grad_side, back in ((S_A, G_A, R_A), (S_B, G_B, R_B)):
        piece(all_of(saved_side))
        gather(saved_side, 0)
        piece(all_of(grad_side))
        gather(grad_side, 1)
        if back == R_A:
            for copy in weight_copies:
                copy.wait()
        piece()
        hidden_bwd()
        rows_bwd(back)
        if back == R_A:
            pick_near(2)

    piece(all_of(X_B))
    gather(X_B, 0)
    piece()
    hidden_fwd()
    rows_fwd(F_B)

    piece(home_of(R_B, range(PARTS[R_B])))
    home_b(0)

    piece(all_of(X_A))
    gather(X_A, 0)
    piece()
    hidden_fwd()
    rows_fwd(F_A)

    piece(home_of(F_B, range(PARTS[F_B])))
    home_b(1)
    piece()
    combine_b(0)
    piece(home_of(R_A, range(PARTS[R_A])))
    combine_a(0)
    for copy in output_copies(0):
        copy.start()
    piece()
    combine_b(1)
    for p in range(PARTS[F_A]):
        piece(home_of(F_A, (p,)))
        combine_a(1, p)
        for copy in output_copies(1, p):
            copy.start()

    shift_g.wait_send()
    shift_x.wait_send()
    for t in range(3):
        crossing(t, lambda copy: copy.wait_send())
    for t in range(2):
        for n in (0, 1):
            y_back_copy(t, n).wait_send()
    for t in RAWS:
        for n in (0, 1):
            pl.when(on_edge)(lambda: edge_copy(t, n).wait_send())
    for place in range(4):

        @pl.when(q == place)
        def _():
            for link in started[place]:
                for op in link[-DEPTH:]:
                    described(place, op).wait_send()

    for copy in output_copies(0):
        copy.wait()
    for p in range(PARTS[F_A]):
        for copy in output_copies(1, p):
            copy.wait()


def give(from_f, from_b, to_f, to_b, held, load_sem, store_sem):
    loads, stores = [], []
    for n, (source, target) in enumerate(((from_f, to_f), (from_b, to_b))):
        loads.append(pltpu.make_async_copy(source, held.at[n], load_sem.at[n]))
        stores.append(pltpu.make_async_copy(held.at[n], target, store_sem.at[n]))
    for load in loads:
        load.start()
    for load, store in zip(loads, stores):
        load.wait()
        store.start()
    for store in stores:
        store.wait()


def on_device(
    held_fwd, ids_fwd, probs_fwd, saved_in, held_grad, ids_bwd, probs_bwd, w_gate, w_up, w_down
):
    hbm = pl.BlockSpec(memory_space=pl.ANY)
    rows = jax.ShapeDtypeStruct((TOK, D), BF16)
    fwd, grad = pl.pallas_call(
        kernel,
        out_shape=(rows, rows),
        in_specs=[hbm] * 10,
        out_specs=(hbm, hbm),
        scratch_shapes=[
            pltpu.VMEM((TOK, D), BF16),
            pltpu.VMEM((1, TOKENS), jnp.int32),
            pltpu.VMEM((1, TOKENS), BF16),
            pltpu.VMEM((1, TOKENS), jnp.int32),
            pltpu.VMEM((1, TOKENS), BF16),
            pltpu.VMEM((2, TOK, D), BF16),
            pltpu.VMEM((D, HID), BF16),
            pltpu.VMEM((D, HID), BF16),
            pltpu.VMEM((HID, D), BF16),
            pltpu.VMEM((TOK, D), BF16),
            pltpu.VMEM((TOK, D), BF16),
            pltpu.VMEM((3, 2, ROWS, HALF), BF16),
            pltpu.VMEM((2, 2, ROWS, HALF), BF16),
            pltpu.VMEM((3, TOK, D), BF16),
            pltpu.VMEM((3, 2, ROWS, HALF), BF16),
            pltpu.VMEM((6, 10, ROWS, HALF), BF16),
            pltpu.VMEM((4, 19, ROWS, HALF), BF16),
            pltpu.VMEM((2, ALL, D), BF16),
            pltpu.VMEM((2, ALL, HID), BF16),
            pltpu.VMEM((2, ALL, HID), F32),
            pltpu.VMEM((2, TOK, D), F32),
            pltpu.VMEM((2 * ALL, 2 * ALL), BF16),
            pltpu.VMEM((2 * ALL, 2 * ALL), BF16),
            pltpu.SemaphoreType.DMA((3,)),
            pltpu.SemaphoreType.DMA((5,)),
            pltpu.SemaphoreType.DMA((2, 2, 2)),
            pltpu.SemaphoreType.DMA((2,)),
            pltpu.SemaphoreType.DMA((2,)),
            pltpu.SemaphoreType.DMA((5, 2)),
            pltpu.SemaphoreType.DMA((5, 2)),
            pltpu.SemaphoreType.DMA((3,)),
            pltpu.SemaphoreType.DMA((3,)),
            pltpu.SemaphoreType.DMA((3, 2)),
            pltpu.SemaphoreType.DMA((3, 2)),
            pltpu.SemaphoreType.DMA((6, 2, STEPS)),
            pltpu.SemaphoreType.DMA((6, 10)),
            pltpu.SemaphoreType.DMA((4, 2, 2, STEPS)),
            pltpu.SemaphoreType.DMA((4, 2, 19)),
        ],
        compiler_params=pltpu.CompilerParams(
            collective_id=0, has_side_effects=True, vmem_limit_bytes=60 * 2**20
        ),
        cost_estimate=pl.CostEstimate(
            flops=7_050_000_000, bytes_accessed=12_000_000, transcendentals=300_000
        ),
        name="relay_experts",
    )(
        held_fwd[0],
        held_grad[0],
        saved_in[0],
        ids_fwd,
        probs_fwd,
        ids_bwd,
        probs_bwd,
        w_gate[0],
        w_up[0],
        w_down[0],
    )
    fwd, grad = pl.pallas_call(
        give,
        out_shape=(rows, rows),
        in_specs=[hbm, hbm],
        out_specs=(hbm, hbm),
        scratch_shapes=[
            pltpu.VMEM((2, TOK, D), BF16),
            pltpu.SemaphoreType.DMA((2,)),
            pltpu.SemaphoreType.DMA((2,)),
        ],
        name="give",
    )(fwd, grad)
    return (fwd[None], grad[None])


def solution(mesh):
    return jax.shard_map(
        on_device,
        mesh=mesh,
        in_specs=(
            P("pipe", "expert", None),
            P("pipe", None),
            P("pipe", None),
            P("pipe", "expert", None),
            P("pipe", "expert", None),
            P("pipe", None),
            P("pipe", None),
            P("pipe", None, "expert"),
            P("pipe", None, "expert"),
            P("pipe", "expert", None),
        ),
        out_specs=(P("pipe", "expert", None), P("pipe", "expert", None)),
        check_vma=False,
    )
```
